32 devices in a mesh: slab: 2 (over x), acq: 8 (over z, core), rng: 2 (over y).
Axes of the slice: x: 2, y: 2, z: 4, core: 2. Of those that a mesh axis runs over, the one named last changes fastest.
Arguments:
- slc: bfloat16 [2, 8, 2, 16, 65536], P(None, 'acq', None, 'slab', 'rng'), parts along dimension 3
- partners: int32 [2, 8, 4], P(None, 'acq'), may hold values from -1 to 15, as said below
- looks: int32 [2, 8, 4], P(None, 'acq'), may hold values from 6 to 10, as said below
Outputs:
- interferogram: bfloat16 [2, 8, 4, 2, 16, 65536], P(None, 'acq', None, None, 'slab', 'rng'), parts along dimension 4
- coherence: bfloat16 [2, 8, 4, 16, 65536], P(None, 'acq', None, 'slab', 'rng'), parts along dimension 3
The draws below stay inside these ranges and needn't reach their ends.
There are 2 independent parts, one for each index of `slab`. The reference program is written for one: setup_inputs(seed, part) draws one part's arguments, and reference() takes and returns one part's arrays. A program takes and returns all parts, laid end to end along the dimension named above; an argument that names none is the same for every part. Nothing has to cross between parts.
Inputs may be any that keep to these rules, and one draw needn't show every extreme that they name: A live partner j of acquisition i satisfies i < j <= i + 8; an acquisition's live partners are distinct; slot 0 of acquisition 0 is live with j = 8, and acquisition 0 fills all 4 slots; empty slots hold -1 and may lie anywhere. `looks`: the largest value is reached in every draw.
All inputs are finite; a program needn't handle non-finite values.
Results may differ from the reference program's by a relative error of at most 0.001.
Values may be sent and summed in bfloat16 or wider, within the bound.
No kernel may reach another device: no remote copies, remote signals or barrier semaphores. Data moves between devices by JAX's collectives and lax.ppermute only.
A program may use at most 192 MiB of HBM per device.

```python
import jax
import jax.numpy as jnp
from jax import lax

RANGE = 65536
LINES = 8
ACQ_DEV = 2
SLOTS = 4
REACH = 8
AZ_HALF = 2
RG_HALF = 10
N_ACQ = 8


def draw_slc(key, part):
    key = jax.random.fold_in(key, 11)
    k_base, k_noise, k_mix = jax.random.split(key, 3)
    base = jax.random.normal(k_base, (2, LINES, RANGE), jnp.float32)
    noise = jax.random.normal(k_noise, (ACQ_DEV, N_ACQ, 2, LINES, RANGE), jnp.float32)
    mixing = jax.random.uniform(k_mix, (ACQ_DEV, N_ACQ, 1, 1, 1), jnp.float32, 0.3, 0.9)
    values = mixing * base[None, None] + jnp.sqrt(1.0 - mixing * mixing) * noise
    return values.astype(jnp.bfloat16)


def draw_partners(key, part):
    key = jax.random.fold_in(key, 12)
    k_score, k_count = jax.random.split(key)
    acqs = ACQ_DEV * N_ACQ
    scores = jax.random.randint(k_score, (acqs, REACH), 0, 1 << 20) * REACH + jnp.arange(REACH, dtype=jnp.int32)[None]
    scores = scores.at[0, REACH - 1].set(jnp.int32(1 << 30))
    order = lax.top_k(scores, SLOTS)[1].astype(jnp.int32)
    counts = jax.random.randint(k_count, (acqs,), 1, SLOTS + 1).at[0].set(SLOTS)
    ids = jnp.arange(acqs, dtype=jnp.int32)[:, None]
    targets = ids + order + 1
    live = (jnp.arange(SLOTS, dtype=jnp.int32)[None] < counts[:, None]) & (targets < acqs)
    return jnp.where(live, targets, -1).astype(jnp.int32).reshape(ACQ_DEV, N_ACQ, SLOTS)


def draw_looks(key, part):
    key = jax.random.fold_in(key, 13)
    k_val, k_pos = jax.random.split(key)
    values = jax.random.randint(k_val, (ACQ_DEV * N_ACQ * SLOTS,), 6, RG_HALF + 1)
    where_top = jax.random.randint(k_pos, (), 0, ACQ_DEV * N_ACQ * SLOTS)
    values = values.at[where_top].set(RG_HALF)
    return values.astype(jnp.int32).reshape(ACQ_DEV, N_ACQ, SLOTS)


def setup_inputs(seed: int = 0, part: int = 0) -> dict:
    key_of = jax.random.split(jax.random.key(seed), 4)
    part_splits = jax.random.split(jax.random.fold_in(key_of[3], part), 4)
    return {
        "slc": draw_slc(jax.random.fold_in(jax.random.fold_in(key_of[3], part), 71), part),
        "partners": draw_partners(jax.random.fold_in(key_of[3], 71), part),
        "looks": draw_looks(jax.random.fold_in(key_of[3], 71), part),
    }


def window_sums(fields, widths):
    lines = fields.shape[2]
    cols = fields.shape[3]
    padded = jnp.pad(fields, ((0, 0), (0, 0), (AZ_HALF, AZ_HALF), (RG_HALF, RG_HALF)))
    along = padded[:, :, 0:lines]
    for step in range(1, 2 * AZ_HALF + 1):
        along = along + padded[:, :, step:step + lines]
    total = jnp.zeros(fields.shape, jnp.float32)
    for offset in range(2 * RG_HALF + 1):
        weight = (jnp.abs(offset - RG_HALF) <= widths).astype(jnp.float32)
        total = total + along[:, :, :, offset:offset + cols] * weight[:, None, None, None]
    return total

def reference(slc, partners, looks):
    acqs = slc.shape[0] * slc.shape[1]
    stack = slc.reshape(acqs, 2, slc.shape[3], slc.shape[4])
    pairs = partners.reshape(acqs, SLOTS)
    widths = looks.reshape(acqs, SLOTS)

    def one_row(index):
        own = stack[index].astype(jnp.float32)
        targets = pairs[index]
        other = jnp.take(stack, jnp.clip(targets, 0, acqs - 1), axis=0).astype(jnp.float32)
        own_re = own[0][None]
        own_im = own[1][None]
        fields = jnp.stack([own_re * other[:, 0] + own_im * other[:, 1], own_im * other[:, 0] - own_re * other[:, 1], jnp.broadcast_to(own_re * own_re + own_im * own_im, other[:, 0].shape), other[:, 0] * other[:, 0] + other[:, 1] * other[:, 1]], axis=1)
        sums = window_sums(fields, widths[index])
        count = ((2 * AZ_HALF + 1) * (2 * widths[index] + 1)).astype(jnp.float32)
        live = (targets >= 0)[:, None, None, None]
        mean_part = jnp.where(live, sums[:, 0:2] / count[:, None, None, None], 0.0)
        magnitude = jnp.sqrt(sums[:, 0] * sums[:, 0] + sums[:, 1] * sums[:, 1])
        ratio = magnitude / jnp.sqrt(sums[:, 2] * sums[:, 3] + 1e-06)
        ratio = jnp.where(live[:, 0], ratio, 0.0)
        return (mean_part.astype(jnp.bfloat16), ratio.astype(jnp.bfloat16))
    result_ifg, result_coh = lax.map(one_row, jnp.arange(acqs, dtype=jnp.int32))
    shape_head = (slc.shape[0], slc.shape[1], SLOTS)
    return (result_ifg.reshape(shape_head + result_ifg.shape[2:]), result_coh.reshape(shape_head + result_coh.shape[2:]))
```

```python
import functools

import jax
import jax.numpy as jnp
from jax import lax
from jax.experimental import pallas as pl
from jax.experimental.pallas import tpu as pltpu
from jax.sharding import PartitionSpec as P

SLOTS = 4
AZ_HALF = 2
HALO = 128
TILE = 256
ROWS = 32
GROUP = 8
TINY = 1e-37


def azimuth(field):
    lines = field.shape[0]
    line = lax.broadcasted_iota(jnp.int32, field.shape, 0)
    total = field
    for step in range(1, AZ_HALF + 1):
        before = jnp.where(line >= step, pltpu.roll(field, step, 0), 0.0)
        after = jnp.where(line < lines - step, pltpu.roll(field, lines - step, 0), 0.0)
        total = total + (before + after)
    return total


def split_sums(own_re, own_im, other_re, other_im):
    fields = (
        own_re * other_re + own_im * other_im,
        own_im * other_re - own_re * other_im,
        own_re * own_re + own_im * own_im,
        other_re * other_re + other_im * other_im,
    )
    sums = jnp.concatenate([azimuth(field) for field in fields], axis=0)
    high = sums.astype(jnp.bfloat16)
    low = (sums - high.astype(jnp.float32)).astype(jnp.bfloat16)
    return high, low


def bands(width):
    row = lax.broadcasted_iota(jnp.int32, (TILE, TILE), 0)
    col = lax.broadcasted_iota(jnp.int32, (TILE, TILE), 1)
    main = jnp.abs(row - col) <= width
    lane = row % HALO
    place = jnp.where(lane >= HALO // 2, lane - HALO, TILE + lane)
    edge = jnp.abs(place - col) <= width
    as_type = lambda mask: jnp.where(mask, 1.0, 0.0).astype(jnp.bfloat16)
    return as_type(main), as_type(edge)


def pair_kernel(
    targets, widths, own, other, own_halo, other_halo, ifg, coh, high, low, main_band, edge_band
):
    pair = pl.program_id(0)
    live = targets[pair] >= 0
    width = widths[pair]
    span = own.shape[-1]
    tiles = span // TILE

    @pl.when(jnp.logical_not(live))
    def _():
        ifg[...] = jnp.zeros_like(ifg)
        coh[...] = jnp.zeros_like(coh)

    @pl.when(live)
    def _():
        main_band[...], edge_band[...] = bands(width)
        f32 = jnp.float32
        for side, tile, lanes in ((0, 0, slice(HALO, TILE)), (1, tiles + 1, slice(0, HALO))):
            parts = [
                ref[0, side, part].astype(f32)
                for ref in (own_halo, other_halo)
                for part in (0, 1)
            ]
            high[tile, :, lanes], low[tile, :, lanes] = split_sums(*parts)

        def fill(tile, carry):
            cols = pl.ds(pl.multiple_of(tile * TILE, TILE), TILE)
            parts = [ref[0, part, :, cols].astype(f32) for ref in (own, other) for part in (0, 1)]
            high[tile + 1], low[tile + 1] = split_sums(*parts)
            return carry

        lax.fori_loop(0, tiles, fill, 0, unroll=4)
        count = jnp.full((8, TILE), (2 * AZ_HALF + 1) * (2 * width + 1), jnp.int32)
        scale = 1.0 / count.astype(f32)
        group = min(GROUP, tiles)
        upper = lax.broadcasted_iota(jnp.int32, (group, ROWS, HALO), 2) >= HALO // 2

        def edges(ref, first):
            left = ref[pl.ds(first, group), :, HALO:]
            right = ref[pl.ds(first + 2, group), :, :HALO]
            return jnp.where(upper, left, right)

        def finish(step, carry):
            first = step * group
            rows = group * ROWS
            edge = jnp.concatenate([edges(high, first), edges(low, first)], axis=-1)
            total = (
                jnp.dot(
                    high[pl.ds(first + 1, group)].reshape(rows, TILE),
                    main_band[...],
                    preferred_element_type=f32,
                )
                + jnp.dot(
                    low[pl.ds(first + 1, group)].reshape(rows, TILE),
                    main_band[...],
                    preferred_element_type=f32,
                )
                + jnp.dot(
                    edge.reshape(rows, TILE), edge_band[...], preferred_element_type=f32
                )
            )
            total = total.reshape(group, 4, ROWS // 4, TILE)
            for tile in range(group):
                real, imag, power, other_power = (total[tile, field] for field in range(4))
                cols = pl.ds(pl.multiple_of((first + tile) * TILE, TILE), TILE)
                ifg[0, 0, 0, :, cols] = (real * scale).astype(jnp.bfloat16)
                ifg[0, 0, 1, :, cols] = (imag * scale).astype(jnp.bfloat16)
                square = real * real + imag * imag
                size = square * lax.rsqrt(jnp.maximum(square, TINY))
                ratio = size * lax.rsqrt(power * other_power + 1e-06)
                coh[0, 0, :, cols] = ratio.astype(jnp.bfloat16)
            return carry

        lax.fori_loop(0, tiles // group, finish, 0)


def pair_products(slc, store, own_halo, halo, targets, widths):
    held, lines, span = slc.shape[0], slc.shape[2], slc.shape[3]
    last = store.shape[0] - 1
    tiles = span // TILE
    pick = lambda pair, targets: jnp.clip(targets[pair], 0, last)
    own_map = lambda pair, targets, widths: (pair // SLOTS, 0, 0, 0)
    other_map = lambda pair, targets, widths: (pick(pair, targets), 0, 0, 0)
    out_map = lambda pair, targets, widths: (pair // SLOTS, pair % SLOTS, 0, 0, 0)
    return pl.pallas_call(
        pair_kernel,
        grid_spec=pltpu.PrefetchScalarGridSpec(
            num_scalar_prefetch=2,
            grid=(held * SLOTS,),
            in_specs=[
                pl.BlockSpec((1, 2, lines, span), own_map),
                pl.BlockSpec((1, 2, lines, span), other_map),
                pl.BlockSpec(
                    (1, 2, 2, lines, HALO), lambda p, t, w: own_map(p, t, w) + (0,)
                ),
                pl.BlockSpec(
                    (1, 2, 2, lines, HALO), lambda p, t, w: other_map(p, t, w) + (0,)
                ),
            ],
            out_specs=[
                pl.BlockSpec((1, 1, 2, lines, span), out_map),
                pl.BlockSpec((1, 1, lines, span), lambda p, t, w: out_map(p, t, w)[:4]),
            ],
            scratch_shapes=[
                pltpu.VMEM((tiles + 2, ROWS, TILE), jnp.bfloat16),
                pltpu.VMEM((tiles + 2, ROWS, TILE), jnp.bfloat16),
                pltpu.VMEM((TILE, TILE), jnp.bfloat16),
                pltpu.VMEM((TILE, TILE), jnp.bfloat16),
            ],
        ),
        out_shape=[
            jax.ShapeDtypeStruct((held, SLOTS, 2, lines, span), jnp.bfloat16),
            jax.ShapeDtypeStruct((held, SLOTS, lines, span), jnp.bfloat16),
        ],
        compiler_params=pltpu.CompilerParams(vmem_limit_bytes=48 * 1024 * 1024),
        name="pair_products",
    )(targets, widths, slc, store, own_halo, halo)


def shards(slc, partners, looks):
    count = lax.axis_size("rng")
    forward = [(i, i + 1) for i in range(count - 1)]
    backward = [(target, source) for source, target in forward]
    low = lax.ppermute(slc[..., -HALO:], "rng", forward)
    high = lax.ppermute(slc[..., :HALO], "rng", backward)
    own_halo = jnp.stack([low, high], axis=2)
    halo = lax.all_gather(own_halo, "acq", axis=1, tiled=True)
    store = lax.all_gather(slc, "acq", axis=1, tiled=True)
    halo = halo.reshape((-1,) + halo.shape[2:])
    store = store.reshape((-1,) + store.shape[2:])
    ifg, coh = pair_products(
        slc[:, 0],
        store,
        own_halo[:, 0],
        halo,
        partners.reshape(-1),
        looks.reshape(-1),
    )
    return ifg[:, None], coh[:, None]


def solution(mesh):
    return jax.shard_map(
        shards,
        mesh=mesh,
        in_specs=(P(None, "acq", None, "slab", "rng"), P(None, "acq", None), P(None, "acq", None)),
        out_specs=(P(None, "acq", None, None, "slab", "rng"), P(None, "acq", None, "slab", "rng")),
        check_vma=False,
    )
```

```python
import functools

import jax
import jax.numpy as jnp
from jax import lax
from jax.experimental import pallas as pl
from jax.experimental.pallas import tpu as pltpu
from jax.sharding import PartitionSpec as P

SLOTS = 4
AZ_HALF = 2
HALO = 128
TILE = 256
ROWS = 32
GROUP = 64
TINY = 1e-37
PER_ROUND = 1
FIXED_ROUNDS = 7
NEVER = 1e6
SEND, GET, TURN, READY, ROUNDS = 0, 2, 4, 5, 6
VMEM = pl.BlockSpec(memory_space=pltpu.VMEM)
SMEM = pl.BlockSpec(memory_space=pltpu.SMEM)
ANYWHERE = pl.BlockSpec(memory_space=pltpu.HBM)
VMEM_LIMIT = 28 * 1024 * 1024


def azimuth(field):
    lines = field.shape[0]
    line = lax.broadcasted_iota(jnp.int32, field.shape, 0)
    total = field
    for step in range(1, AZ_HALF + 1):
        before = jnp.where(line >= step, pltpu.roll(field, step, 0), 0.0)
        after = jnp.where(line < lines - step, pltpu.roll(field, lines - step, 0), 0.0)
        total = total + (before + after)
    return total


def split_sums(own_re, own_im, other_re, other_im):
    fields = (
        own_re * other_re + own_im * other_im,
        own_im * other_re - own_re * other_im,
        own_re * own_re + own_im * own_im,
        other_re * other_re + other_im * other_im,
    )
    sums = jnp.concatenate([azimuth(field) for field in fields], axis=0)
    high = sums.astype(jnp.bfloat16)
    low = (sums - high.astype(jnp.float32)).astype(jnp.bfloat16)
    return high, low


def bands(width):
    row = lax.broadcasted_iota(jnp.int32, (TILE, TILE), 0)
    col = lax.broadcasted_iota(jnp.int32, (TILE, TILE), 1)
    main = jnp.abs(row - col) <= width
    lane = row % HALO
    place = jnp.where(lane >= HALO // 2, lane - HALO, TILE + lane)
    edge = jnp.abs(place - col) <= width
    as_type = lambda mask: jnp.where(mask, 1.0, 0.0).astype(jnp.bfloat16)
    return as_type(main), as_type(edge)


def pair_sums(width, own, other, ifg, coh, high, low, main_band, edge_band, acc, settle=None):
    f32 = jnp.float32
    span = own.shape[-1] - 2 * HALO
    tiles = span // TILE
    main_band[...], edge_band[...] = bands(width)

    def loaded(cols):
        return [ref[part, :, cols].astype(f32) for ref in (own, other) for part in (0, 1)]

    high[0, :, HALO:], low[0, :, HALO:] = split_sums(*loaded(slice(0, HALO)))
    high[tiles + 1, :, :HALO], low[tiles + 1, :, :HALO] = split_sums(
        *loaded(slice(HALO + span, 2 * HALO + span))
    )

    def fill(tile, carry):
        cols = pl.ds(pl.multiple_of(tile * TILE + HALO, HALO), TILE)
        high[tile + 1], low[tile + 1] = split_sums(*loaded(cols))
        return carry

    lax.fori_loop(0, tiles, fill, 0, unroll=4)
    if settle is not None:
        settle()
    count = jnp.full((8, TILE), (2 * AZ_HALF + 1) * (2 * width + 1), jnp.int32)
    scale = 1.0 / count.astype(f32)
    group = min(GROUP, tiles)
    steps = tiles // group
    upper = lax.broadcasted_iota(jnp.int32, (group, ROWS, HALO), 2) >= HALO // 2
    dot = functools.partial(jnp.dot, preferred_element_type=f32)

    def edges(ref, first):
        left = ref[pl.ds(first, group), :, HALO:]
        right = ref[pl.ds(first + 2, group), :, :HALO]
        return jnp.where(upper, left, right)

    def spread(step):
        first = step * group
        rows = group * ROWS
        edge = jnp.concatenate([edges(high, first), edges(low, first)], axis=-1)
        total = (
            dot(high[pl.ds(first + 1, group)].reshape(rows, TILE), main_band[...])
            + dot(low[pl.ds(first + 1, group)].reshape(rows, TILE), main_band[...])
            + dot(edge.reshape(rows, TILE), edge_band[...])
        )
        acc[...] = total.reshape(group, ROWS, TILE)

    def finish(step):
        def one(tile, carry):
            total = acc[tile]
            real, imag, power, other_power = (total[8 * field:8 * field + 8] for field in range(4))
            cols = pl.ds(pl.multiple_of((step * group + tile) * TILE, TILE), TILE)
            ifg[0, :, cols] = (real * scale).astype(jnp.bfloat16)
            ifg[1, :, cols] = (imag * scale).astype(jnp.bfloat16)
            square = real * real + imag * imag
            size = square * lax.rsqrt(jnp.maximum(square, TINY))
            ratio = size * lax.rsqrt(power * other_power + 1e-06)
            coh[:, cols] = ratio.astype(jnp.bfloat16)
            return carry
        lax.fori_loop(0, group, one, 0, unroll=4)

    def both_steps(step, carry):
        spread(step)
        finish(step)
        return carry
    lax.fori_loop(0, steps, both_steps, 0)


def prepare_kernel(
    devices, table, position, own, own_edges, sibling, sibling_edges, store, plan, send, after,
    ifg, coh, sems,
):
    me = position[0]
    chip, core = me // 2, me % 2
    held, span = own.shape[0], own.shape[-1]
    slots = held * SLOTS
    copies = []
    for index in range(held):
        for image, edges, owner in (
            (own, own_edges, me),
            (sibling, sibling_edges, me + 1 - 2 * core),
        ):
            place = store.at[index * devices + owner]
            for source, start, size in (
                (image.at[index], HALO, span),
                (edges.at[index, 0], 0, HALO),
                (edges.at[index, 1], HALO + span, HALO),
            ):
                copies.append(
                    pltpu.make_async_copy(
                        source, place.at[:, :, pl.ds(start, size)], sems.at[len(copies)]
                    )
                )
    for copy in copies:
        copy.start()

    f32 = jnp.float32
    shape = (8, 128)
    row = lax.broadcasted_iota(jnp.int32, shape, 0)
    lane = lax.broadcasted_iota(jnp.int32, shape, 1)
    rowf, lanef = row.astype(f32), lane.astype(f32)
    home = ((lane % devices) // 2).astype(f32)
    nearest = jnp.full(shape, NEVER, f32)
    farthest = jnp.full(shape, -1.0, f32)
    for block in range(devices):
        holder = jnp.full(shape, (me ^ block) // 2, jnp.int32).astype(f32)
        hit = jnp.zeros(shape, jnp.bool_)
        for entry in range(slots):
            line, slot = block * held + entry // SLOTS, entry % SLOTS
            hit = hit | (lane == table[line, slot])
        nearest = jnp.where(hit, jnp.minimum(nearest, holder), nearest)
        farthest = jnp.where(hit, jnp.maximum(farthest, holder), farthest)
    need_down = (nearest < rowf) & (rowf <= home)
    need_up = (home < rowf) & (rowf <= farthest)
    key_down = nearest * 128 + lanef
    key_up = (devices - farthest) * 128 + lanef

    def move(need, key, ready, turn, items, now, towards):
        open_key = jnp.where(ready <= now, key, NEVER)
        best = jnp.min(open_key, axis=1, keepdims=True)
        chosen = (open_key == best) & (open_key < NEVER)
        item = jnp.max(jnp.where(chosen, lanef, -1.0), axis=1, keepdims=True)
        items = jnp.where(lanef == now, item, items)
        turn = jnp.where(chosen, now, turn)
        later = pltpu.roll(jnp.where(chosen, now + 2, NEVER), towards, 0)
        ready = jnp.where(chosen, NEVER, ready)
        ready = jnp.where(need, jnp.minimum(ready, later), ready)
        return ready, turn, items

    def advance(state):
        now, _, ready_down, turn_down, items_down, ready_up, turn_up, items_up = state
        ready_down, turn_down, items_down = move(
            need_down, key_down, ready_down, turn_down, items_down, now, 7
        )
        ready_up, turn_up, items_up = move(
            need_up, key_up, ready_up, turn_up, items_up, now, 1
        )
        soonest = jnp.min(jnp.minimum(ready_down, ready_up))
        return (now + 1.0, soonest) + (
            ready_down, turn_down, items_down, ready_up, turn_up, items_up
        )

    none = jnp.full(shape, -1.0, f32)
    ready_down = jnp.where(need_down & (rowf == home), 0.0, NEVER)
    ready_up = jnp.where(need_up & (rowf == home + 1), 0.0, NEVER)
    soonest = jnp.min(jnp.minimum(ready_down, ready_up))
    rounds, _, _, turn_down, items_down, _, turn_up, items_up = lax.while_loop(
        lambda state: state[1] < NEVER,
        advance,
        (jnp.float32(0.0), soonest, ready_down, none, none, ready_up, none, none),
    )

    def line_of(values, index):
        return jnp.max(jnp.where(row == index, values, -1.0), axis=0, keepdims=True)

    send_down, get_down = line_of(items_down, chip), line_of(items_down, chip + 1)
    send_up, get_up = line_of(items_up, chip + 1), line_of(items_up, chip)
    down_turn, up_turn = line_of(turn_down, chip + 1), line_of(turn_up, chip)
    lag = lambda turn, mine: jnp.where(turn >= 0, turn + jnp.where(mine, 1.0, 2.0), 0.0)
    arrival = jnp.maximum(lag(down_turn, core == 0), lag(up_turn, core == 1))
    partner = jnp.full(shape, -1, jnp.int32)
    for slot in range(slots):
        partner = jnp.where(row == slot, table[slot // SLOTS, slot % SLOTS], partner)
    ready = jnp.max(jnp.where(lane == partner, arrival, 0.0), axis=1, keepdims=True)
    ready = jnp.broadcast_to(ready, shape)

    def turned(values):
        return jnp.sum(jnp.where(row == lane, values, 0.0), axis=0, keepdims=True)

    ready_q = turned(ready)
    live_q = turned(jnp.where(partner >= 0, 1.0, 0.0)) > 0
    ahead = (ready_q < ready) | ((ready_q == ready) & (lane < row))
    rank = jnp.sum(jnp.where(ahead & live_q, 1.0, 0.0), axis=1, keepdims=True)
    rank = jnp.broadcast_to(rank, shape)
    gap = (rank - turned(rank)) / PER_ROUND
    whole = jnp.floor(gap)
    queue = (gap >= 0) & (gap == whole) & live_q
    turn = jnp.max(jnp.where(queue, ready_q + whole, 0.0), axis=1, keepdims=True)
    turn = turned(jnp.where(partner >= 0, turn, (row % SLOTS).astype(f32)))
    result = jnp.full(shape, rounds, f32)
    for index, values in enumerate([send_down, send_up, get_down, get_up, turn, ready_q]):
        result = jnp.where(row == index, values, result)
    plan[...] = result.astype(jnp.int32)

    for copy in copies:
        copy.wait()
    sends = []
    for index, block in enumerate((send, after)):
        mine = jnp.where(core == 0, send_down, send_up)
        item = jnp.max(jnp.where(lane[:1] == index, mine, -1.0)).astype(jnp.int32)
        sends.append(
            pltpu.make_async_copy(
                store.at[jnp.where(item < 0, me, item)], block, sems.at[index]
            )
        )
    for copy in sends:
        copy.start()
    for copy in sends:
        copy.wait()


def prepare(own, own_edges, sibling, sibling_edges, table, position, devices):
    held, parts, lines, span = own.shape
    bf16 = jnp.bfloat16
    item = jax.ShapeDtypeStruct((parts, lines, span + 2 * HALO), bf16)
    return pl.pallas_call(
        functools.partial(prepare_kernel, devices),
        in_specs=[SMEM, SMEM, VMEM, VMEM, VMEM, VMEM],
        out_specs=[ANYWHERE, VMEM, VMEM, VMEM] + [ANYWHERE] * 2,
        scratch_shapes=[pltpu.SemaphoreType.DMA((6 * held,))],
        out_shape=[
            jax.ShapeDtypeStruct((held * devices,) + item.shape, bf16),
            jax.ShapeDtypeStruct((8, 128), jnp.int32),
            item,
            item,
            jax.ShapeDtypeStruct((held, SLOTS, parts, lines, span), bf16),
            jax.ShapeDtypeStruct((held, SLOTS, lines, span), bf16),
        ],
        compiler_params=pltpu.CompilerParams(vmem_limit_bytes=VMEM_LIMIT),
        name="prepare",
    )(table, position, own, own_edges, sibling, sibling_edges)


def pair_kernel(devices, placing, plan, targets, widths, step, _store, *refs):
    swapped = None
    if placing:
        swapped, *refs = refs
    (
        _ifg, _coh, store, ifg, coh, own, other, ifg_block, coh_block, high, low, main_band,
        edge_band, acc, sems,
    ) = refs
    first, after, ready_above, ready_up_to, now, me = (step[index] for index in range(6))
    slots = ifg.shape[0] * SLOTS
    if placing:
        item = jnp.where(now > 0, plan[GET + 1 - me % 2, jnp.maximum(now - 1, 0)], -1)

        @pl.when(item >= 0)
        def _():
            place = pltpu.make_async_copy(swapped, store.at[item], sems.at[0])
            place.start()
            place.wait()

    def results(pair):
        held, slot = pair // SLOTS, pair % SLOTS
        return (
            pltpu.make_async_copy(ifg_block, ifg.at[held, slot], sems.at[2]),
            pltpu.make_async_copy(coh_block, coh.at[held, slot], sems.at[3]),
        )

    def settle(last):
        @pl.when(last >= 0)
        def _():
            for copy in results(jnp.maximum(last, 0)):
                copy.wait()

    def serve(pair, last):
        turn, ready = plan[TURN, pair], plan[READY, pair]
        due = (turn >= first) & (turn < after) & (ready > ready_above) & (ready <= ready_up_to)

        @pl.when(due)
        def _():
            held, slot = pair // SLOTS, pair % SLOTS
            target = targets[held, slot]

            @pl.when(target < 0)
            def _():
                settle(last)
                ifg_block[...] = jnp.zeros_like(ifg_block)
                coh_block[...] = jnp.zeros_like(coh_block)

            @pl.when(target >= 0)
            def _():
                loads = (
                    pltpu.make_async_copy(store.at[held * devices + me], own, sems.at[0]),
                    pltpu.make_async_copy(store.at[target], other, sems.at[1]),
                )
                for load in loads:
                    load.start()
                for load in loads:
                    load.wait()
                pair_sums(
                    widths[held, slot], own, other, ifg_block, coh_block, high, low, main_band,
                    edge_band, acc, functools.partial(settle, last),
                )

            for copy in results(pair):
                copy.start()

        return jnp.where(due, pair, last)

    settle(lax.fori_loop(0, slots, serve, jnp.int32(-1)))


def like(array):
    return jax.ShapeDtypeStruct(array.shape, array.dtype)


def pair_work(plan, targets, widths, step, store, swapped, ifg, coh, devices):
    parts, lines, span = store.shape[1:]
    width = span - 2 * HALO
    tiles = width // TILE
    bf16 = jnp.bfloat16
    extra = [] if swapped is None else [swapped]
    placing = len(extra)
    return pl.pallas_call(
        functools.partial(pair_kernel, devices, bool(placing)),
        in_specs=[SMEM] * 4 + [ANYWHERE] + [VMEM] * placing + [ANYWHERE, ANYWHERE],
        out_specs=[ANYWHERE] * 3,
        scratch_shapes=[
            pltpu.VMEM((parts, lines, span), bf16),
            pltpu.VMEM((parts, lines, span), bf16),
            pltpu.VMEM((parts, lines, width), bf16),
            pltpu.VMEM((lines, width), bf16),
            pltpu.VMEM((tiles + 2, ROWS, TILE), bf16),
            pltpu.VMEM((tiles + 2, ROWS, TILE), bf16),
            pltpu.VMEM((TILE, TILE), bf16),
            pltpu.VMEM((TILE, TILE), bf16),
            pltpu.VMEM((min(GROUP, tiles), ROWS, TILE), jnp.float32),
            pltpu.SemaphoreType.DMA((4,)),
        ],
        out_shape=[like(store), like(ifg), like(coh)],
        input_output_aliases={4: 0, 5 + placing: 1, 6 + placing: 2},
        compiler_params=pltpu.CompilerParams(vmem_limit_bytes=VMEM_LIMIT),
        cost_estimate=pl.CostEstimate(
            flops=10_000_000_000, bytes_accessed=8_000_000, transcendentals=0
        ),
        name="pair_work",
    )(plan, targets, widths, step, store, *extra, ifg, coh)


def forward_kernel(ahead, keep, plan, step, _store, new, swapped, store, following, *refs):
    sems = refs[-1]
    now, core = step[4], step[5] % 2
    item, sent = plan[GET + core, now], plan[SEND + core, now + ahead]
    late = jnp.where(now > 0, plan[GET + 1 - core, jnp.maximum(now - 1, 0)], -1)
    moves = (
        (item >= 0, new, item, True),
        (late >= 0, swapped, late, True),
        ((sent >= 0) & (sent != item), following, sent, False),
    )

    def each(act):
        for index, (wanted, block, place, out) in enumerate(moves):

            @pl.when(wanted)
            def _():
                ends = (block, store.at[place]) if out else (store.at[place], block)
                act(pltpu.make_async_copy(*ends, sems.at[index]))

    each(lambda copy: copy.start())
    if keep:
        refs[0][...] = new[...]

    @pl.when((sent >= 0) & (sent == item))
    def _():
        following[...] = new[...]

    each(lambda copy: copy.wait())


def forward(plan, step, store, new, swapped, ahead, keep):
    return pl.pallas_call(
        functools.partial(forward_kernel, ahead, keep),
        in_specs=[SMEM] * 2 + [ANYWHERE, VMEM, VMEM],
        out_specs=[ANYWHERE, VMEM] + [VMEM] * keep,
        scratch_shapes=[pltpu.SemaphoreType.DMA((3,))],
        out_shape=[like(store)] + [like(new)] * (1 + keep),
        input_output_aliases={2: 0},
        compiler_params=pltpu.CompilerParams(vmem_limit_bytes=VMEM_LIMIT),
        name="forward",
    )(plan, step, store, new, swapped)


def shards(slc, partners, looks):
    devices = lax.axis_size("acq")
    me = lax.axis_index("acq").astype(jnp.int32)
    swap = [(d, d ^ 1) for d in range(devices)]
    stream = [(d, d - 2) for d in range(2, devices, 2)] + [(d, d + 2) for d in range(1, devices - 2, 2)]
    own, targets, widths = slc[:, 0], partners[:, 0], looks[:, 0]
    table = targets
    distance = 1
    while distance < devices:
        other = lax.ppermute(table, "acq", [(d, d ^ distance) for d in range(devices)])
        table = jnp.concatenate([table, other])
        distance *= 2

    count = lax.axis_size("rng")
    forth = [(i, i + 1) for i in range(count - 1)]
    back = [(target, source) for source, target in forth]
    before = lax.ppermute(own[..., -HALO:], "rng", forth)
    after = lax.ppermute(own[..., :HALO], "rng", back)
    edges = jnp.stack([before, after], axis=1)
    sibling = lax.ppermute(own, "acq", swap)
    sibling_edges = lax.ppermute(edges, "acq", swap)
    store, plan, send, after, ifg, coh = prepare(
        own, edges, sibling, sibling_edges, table, me[None], devices
    )
    rounds = plan[ROUNDS, 0]
    late = jnp.int32(1 << 20)

    def pairs_of(now, store, ifg, coh):
        step = jnp.stack([jnp.int32(now), jnp.int32(now + 1), -late, late, jnp.int32(now), me])
        return pair_work(plan, targets, widths, step, store, None, ifg, coh, devices)

    def forwarded(now, store, new, swapped, ahead, keep=False):
        step = jnp.stack([jnp.int32(0)] * 4 + [jnp.int32(now), me])
        return forward(plan, step, store, new, swapped, ahead, keep)

    news, swaps, sends = [], [send], [send, after]
    for now in range(FIXED_ROUNDS):
        news.append(lax.ppermute(sends[now], "acq", stream))
        if now > 0:
            store, send = forwarded(now - 1, store, news[now - 1], swaps[now - 1], 2)
            sends.append(send)
            swaps.append(lax.ppermute(news[now - 1], "acq", swap))
        store, ifg, coh = pairs_of(now, store, ifg, coh)
    store, _ = forwarded(FIXED_ROUNDS - 1, store, news[-1], swaps[-1], 2)

    def body(state):
        now, store, send, got, ifg, coh = state
        new = lax.ppermute(send, "acq", stream)
        swapped = lax.ppermute(got, "acq", swap)
        store, ifg, coh = pairs_of(now, store, ifg, coh)
        store, send, got = forwarded(now, store, new, swapped, 1, True)
        return now + 1, store, send, got, ifg, coh

    now, store, _, got, ifg, coh = lax.while_loop(
        lambda state: state[0] < rounds,
        body,
        (jnp.int32(FIXED_ROUNDS), store, sends[-1], news[-1], ifg, coh),
    )
    swapped = lax.ppermute(got, "acq", swap)
    step = jnp.stack([now, late, -late, now, now, me])
    store, ifg, coh = pair_work(plan, targets, widths, step, store, None, ifg, coh, devices)
    step = jnp.stack([now, late, now, late, now, me])
    _, ifg, coh = pair_work(plan, targets, widths, step, store, swapped, ifg, coh, devices)
    return ifg[:, None], coh[:, None]


def solution(mesh):
    return jax.shard_map(
        shards,
        mesh=mesh,
        in_specs=(P(None, "acq", None, "slab", "rng"), P(None, "acq", None), P(None, "acq", None)),
        out_specs=(P(None, "acq", None, None, "slab", "rng"), P(None, "acq", None, "slab", "rng")),
        check_vma=False,
    )
```

```python
import functools

import jax
import jax.numpy as jnp
from jax import lax
from jax.experimental import pallas as pl
from jax.experimental.pallas import tpu as pltpu
from jax.sharding import PartitionSpec as P

SLOTS = 4
AZ_HALF = 2
HALO = 128
TILE = 256
ROWS = 32
GROUP = 16
TINY = 1e-37
PER_ROUND = 1
FIXED_ROUNDS = 7
NEVER = 1e6
SEND, GET, TURN, READY, ROUNDS, TARGET, WIDTH, SELF = 0, 2, 4, 5, 6, 8, 9, 10
VMEM = pl.BlockSpec(memory_space=pltpu.VMEM)
SMEM = pl.BlockSpec(memory_space=pltpu.SMEM)
ANYWHERE = pl.BlockSpec(memory_space=pltpu.HBM)
VMEM_LIMIT = 40 * 1024 * 1024


def azimuth(field):
    lines = field.shape[0]
    line = lax.broadcasted_iota(jnp.int32, field.shape, 0)
    above = jnp.where(line >= 1, pltpu.roll(field, 1, 0), 0.0)
    pair = field + above
    ends = jnp.where(line >= 2, pair, jnp.where(line == 0, pltpu.roll(field, 1, 0), 0.0))
    return (pair + jnp.where(line >= 2, pltpu.roll(field, 2, 0), 0.0)) + pltpu.roll(ends, lines - 2, 0)


def split_sums(own_re, own_im, other_re, other_im):
    fields = (
        own_re * other_re + own_im * other_im,
        own_im * other_re - own_re * other_im,
        own_re * own_re + own_im * own_im,
        other_re * other_re + other_im * other_im,
    )
    sums = jnp.concatenate([azimuth(field) for field in fields], axis=0)
    high = sums.astype(jnp.bfloat16)
    low = (sums - high.astype(jnp.float32)).astype(jnp.bfloat16)
    return high, low


def bands(width):
    row = lax.broadcasted_iota(jnp.int32, (TILE, TILE), 0)
    col = lax.broadcasted_iota(jnp.int32, (TILE, TILE), 1)
    main = jnp.abs(row - col) <= width
    lane = row % HALO
    place = jnp.where(lane >= HALO // 2, lane - HALO, TILE + lane)
    edge = jnp.abs(place - col) <= width
    as_type = lambda mask: jnp.where(mask, 1.0, 0.0).astype(jnp.bfloat16)
    return as_type(main), as_type(edge)


def group_of(tiles):
    return min(GROUP, tiles // 2)


def pair_sums(
    width, own, other, ifg, coh, main_band, edge_band, buffers, arrive, leave
):
    f32, bf16 = jnp.float32, jnp.bfloat16
    span = own.shape[-1] - 2 * HALO
    tiles = span // TILE
    main_band[...], edge_band[...] = bands(width)
    group = group_of(tiles)
    steps = tiles // group
    rows = group * ROWS
    count = jnp.full((8, TILE), (2 * AZ_HALF + 1) * (2 * width + 1), jnp.int32)
    scale = 1.0 / count.astype(f32)
    upper = lax.broadcasted_iota(jnp.int32, (group, ROWS, HALO), 2) >= HALO // 2
    dot = functools.partial(jnp.dot, preferred_element_type=f32)

    def place(start, size):
        return pl.ds(pl.multiple_of(start, HALO), size)

    def loaded(start, size):
        cols = place(start, size)
        return split_sums(
            *(ref[part, :, cols].astype(f32) for ref in (own, other) for part in (0, 1))
        )

    def fill(step, slot):
        high, low = buffers[slot]
        base = step * group * TILE
        high[0, :, HALO:], low[0, :, HALO:] = loaded(base, HALO)
        for tile in range(group):
            high[tile + 1], low[tile + 1] = loaded(base + HALO + tile * TILE, TILE)
        end = loaded(base + HALO + group * TILE, HALO)
        high[group + 1, :, :HALO], low[group + 1, :, :HALO] = end

    def spread(step, slot):
        high, low = buffers[slot]
        edge = jnp.concatenate(
            [jnp.where(upper, ref[:group, :, HALO:], ref[2:, :, :HALO]) for ref in (high, low)],
            axis=-1,
        )
        total = (
            dot(high[1 : group + 1].reshape(rows, TILE), main_band[...])
            + dot(low[1 : group + 1].reshape(rows, TILE), main_band[...])
            + dot(edge.reshape(rows, TILE), edge_band[...])
        ).reshape(group, 4, ROWS // 4, TILE)
        for tile in range(group):
            real, imag, power, other_power = (total[tile, field] for field in range(4))
            cols = place((step * group + tile) * TILE, TILE)
            ifg[0, :, cols] = (real * scale).astype(bf16)
            ifg[1, :, cols] = (imag * scale).astype(bf16)
            square = real * real + imag * imag
            size = square * lax.rsqrt(jnp.maximum(square, TINY))
            ratio = size * lax.rsqrt(power * other_power + 1e-06)
            coh[:, cols] = ratio.astype(bf16)

    def turn(step, slot, more=True):
        if more:
            arrive(step + 1)
            spread(step, slot)
            fill(step + 1, 1 - slot)
        else:
            spread(step, slot)
        leave(step)

    arrive(0)
    fill(0, 0)

    def twice(half, carry):
        turn(2 * half, 0)
        turn(2 * half + 1, 1)
        return carry

    lax.fori_loop(0, steps // 2 - 1, twice, 0)
    turn(steps - 2, 0)
    turn(steps - 1, 1, False)


def prepare_kernel(
    devices, table, widths, position, own_image, own_edges, sibling, sibling_edges, store, plan,
    send, after, ifg, coh, own, zero, load_sem, sems, zero_sems,
):
    me = position[0]
    chip, core = me // 2, me % 2
    held, span = own.shape[0], own.shape[-1]
    slots = held * SLOTS
    load = pltpu.make_async_copy(own_image, own, load_sem)
    load.start()
    zero[...] = jnp.zeros_like(zero)

    def clear(act):
        for slot in range(slots):

            @pl.when(table[slot // SLOTS, slot % SLOTS] < 0)
            def _():
                for ref, source, sem in ((ifg, zero, 0), (coh, zero.at[0], 1)):
                    place = ref.at[slot // SLOTS, slot % SLOTS]
                    act(pltpu.make_async_copy(source, place, zero_sems.at[slot, sem]))

    clear(lambda copy: copy.start())
    copies = []
    for index in range(held):
        for image, edges, owner in (
            (own, own_edges, me),
            (sibling, sibling_edges, me + 1 - 2 * core),
        ):
            place = store.at[index * devices + owner]
            for source, start, size in (
                (image.at[index], HALO, span),
                (edges.at[index, 0], 0, HALO),
                (edges.at[index, 1], HALO + span, HALO),
            ):
                copies.append(
                    pltpu.make_async_copy(
                        source, place.at[:, :, pl.ds(start, size)], sems.at[len(copies)]
                    )
                )
    load.wait()
    for copy in copies:
        copy.start()

    f32 = jnp.float32
    shape = (8, 128)
    row = lax.broadcasted_iota(jnp.int32, shape, 0)
    lane = lax.broadcasted_iota(jnp.int32, shape, 1)
    rowf, lanef = row.astype(f32), lane.astype(f32)
    home = ((lane % devices) // 2).astype(f32)
    nearest = jnp.full(shape, NEVER, f32)
    farthest = jnp.full(shape, -1.0, f32)
    for block in range(devices):
        holder = jnp.full(shape, (me ^ block) // 2, jnp.int32).astype(f32)
        hit = jnp.zeros(shape, jnp.bool_)
        for entry in range(slots):
            line, slot = block * held + entry // SLOTS, entry % SLOTS
            hit = hit | (lane == table[line, slot])
        nearest = jnp.where(hit, jnp.minimum(nearest, holder), nearest)
        farthest = jnp.where(hit, jnp.maximum(farthest, holder), farthest)
    need_down = (nearest < rowf) & (rowf <= home)
    need_up = (home < rowf) & (rowf <= farthest)
    key_down = nearest * 128 + lanef
    key_up = (devices - farthest) * 128 + lanef

    def move(need, key, ready, turn, items, now, towards):
        open_key = jnp.where(ready <= now, key, NEVER)
        best = jnp.min(open_key, axis=1, keepdims=True)
        chosen = (open_key == best) & (open_key < NEVER)
        item = jnp.max(jnp.where(chosen, lanef, -1.0), axis=1, keepdims=True)
        items = jnp.where(lanef == now, item, items)
        turn = jnp.where(chosen, now, turn)
        later = pltpu.roll(jnp.where(chosen, now + 2, NEVER), towards, 0)
        ready = jnp.where(chosen, NEVER, ready)
        ready = jnp.where(need, jnp.minimum(ready, later), ready)
        return ready, turn, items

    def advance(state):
        now, _, ready_down, turn_down, items_down, ready_up, turn_up, items_up = state
        ready_down, turn_down, items_down = move(
            need_down, key_down, ready_down, turn_down, items_down, now, 7
        )
        ready_up, turn_up, items_up = move(
            need_up, key_up, ready_up, turn_up, items_up, now, 1
        )
        soonest = jnp.min(jnp.minimum(ready_down, ready_up))
        return (now + 1.0, soonest) + (
            ready_down, turn_down, items_down, ready_up, turn_up, items_up
        )

    none = jnp.full(shape, -1.0, f32)
    ready_down = jnp.where(need_down & (rowf == home), 0.0, NEVER)
    ready_up = jnp.where(need_up & (rowf == home + 1), 0.0, NEVER)
    soonest = jnp.min(jnp.minimum(ready_down, ready_up))
    rounds, _, _, turn_down, items_down, _, turn_up, items_up = lax.while_loop(
        lambda state: state[1] < NEVER,
        advance,
        (jnp.float32(0.0), soonest, ready_down, none, none, ready_up, none, none),
    )

    def line_of(values, index):
        return jnp.max(jnp.where(row == index, values, -1.0), axis=0, keepdims=True)

    send_down, get_down = line_of(items_down, chip), line_of(items_down, chip + 1)
    send_up, get_up = line_of(items_up, chip + 1), line_of(items_up, chip)
    down_turn, up_turn = line_of(turn_down, chip + 1), line_of(turn_up, chip)
    lag = lambda turn, mine: jnp.where(turn >= 0, turn + jnp.where(mine, 1.0, 2.0), 0.0)
    arrival = jnp.maximum(lag(down_turn, core == 0), lag(up_turn, core == 1))
    partner = jnp.full(shape, -1, jnp.int32)
    for slot in range(slots):
        partner = jnp.where(row == slot, table[slot // SLOTS, slot % SLOTS], partner)
    ready = jnp.max(jnp.where(lane == partner, arrival, 0.0), axis=1, keepdims=True)
    ready = jnp.broadcast_to(ready, shape)

    def turned(values):
        return jnp.sum(jnp.where(row == lane, values, 0.0), axis=0, keepdims=True)

    ready_q = turned(ready)
    live_q = turned(jnp.where(partner >= 0, 1.0, 0.0)) > 0
    ahead = (ready_q < ready) | ((ready_q == ready) & (lane < row))
    rank = jnp.sum(jnp.where(ahead & live_q, 1.0, 0.0), axis=1, keepdims=True)
    rank = jnp.broadcast_to(rank, shape)
    gap = (rank - turned(rank)) / PER_ROUND
    whole = jnp.floor(gap)
    queue = (gap >= 0) & (gap == whole) & live_q
    turn = jnp.max(jnp.where(queue, ready_q + whole, 0.0), axis=1, keepdims=True)
    turn = turned(jnp.where(partner >= 0, turn, -1.0))
    result = jnp.full(shape, rounds, f32)
    for index, values in enumerate([send_down, send_up, get_down, get_up, turn, ready_q]):
        result = jnp.where(row == index, values, result)
    extra = jnp.full(shape, me, jnp.int32)
    for slot in range(slots):
        spot = slot // SLOTS, slot % SLOTS
        extra = jnp.where((row == TARGET - 8) & (lane == slot), table[spot], extra)
        extra = jnp.where((row == WIDTH - 8) & (lane == slot), widths[spot], extra)
    plan[:8] = result.astype(jnp.int32)
    plan[8:] = extra

    for copy in copies:
        copy.wait()
    sends = []
    for index, block in enumerate((send, after)):
        mine = jnp.where(core == 0, send_down, send_up)
        item = jnp.max(jnp.where(lane[:1] == index, mine, -1.0)).astype(jnp.int32)
        sends.append(
            pltpu.make_async_copy(
                store.at[jnp.where(item < 0, me, item)], block, sems.at[index]
            )
        )
    for copy in sends:
        copy.start()
    for copy in sends:
        copy.wait()
    clear(lambda copy: copy.wait())


def prepare(own, own_edges, sibling, sibling_edges, table, widths, position, devices):
    held, parts, lines, span = own.shape
    bf16 = jnp.bfloat16
    item = jax.ShapeDtypeStruct((parts, lines, span + 2 * HALO), bf16)
    return pl.pallas_call(
        functools.partial(prepare_kernel, devices),
        in_specs=[SMEM, SMEM, SMEM, ANYWHERE, VMEM, VMEM, VMEM],
        out_specs=[ANYWHERE, VMEM, VMEM, VMEM] + [ANYWHERE] * 2,
        scratch_shapes=[
            pltpu.VMEM(own.shape, bf16),
            pltpu.VMEM((parts, lines, span), bf16),
            pltpu.SemaphoreType.DMA,
            pltpu.SemaphoreType.DMA((6 * held,)),
            pltpu.SemaphoreType.DMA((held * SLOTS, 2)),
        ],
        out_shape=[
            jax.ShapeDtypeStruct((held * devices,) + item.shape, bf16),
            jax.ShapeDtypeStruct((16, 128), jnp.int32),
            item,
            item,
            jax.ShapeDtypeStruct((held, SLOTS, parts, lines, span), bf16),
            jax.ShapeDtypeStruct((held, SLOTS, lines, span), bf16),
        ],
        compiler_params=pltpu.CompilerParams(vmem_limit_bytes=VMEM_LIMIT),
        name="prepare",
    )(table, widths, position, own, own_edges, sibling, sibling_edges)


def pair_kernel(devices, placing, plan, step, _store, *refs):
    swapped = None
    if placing:
        swapped, *refs = refs
    (
        _ifg, _coh, store, ifg, coh, own, other, ifg_block, coh_block, main_band, edge_band,
        high_even, low_even, high_odd, low_odd, place_sem, in_sems, out_sems,
    ) = refs
    first, after, ready_above, ready_up_to, now = (step[index] for index in range(5))
    me = plan[SELF, 0]
    slots = ifg.shape[0] * SLOTS
    tiles = ifg.shape[-1] // TILE
    piece = group_of(tiles) * TILE
    pieces = tiles * TILE // piece
    if placing:
        item = jnp.where(now > 0, plan[GET + 1 - me % 2, jnp.maximum(now - 1, 0)], -1)

        @pl.when(item >= 0)
        def _():
            place = pltpu.make_async_copy(swapped, store.at[item], place_sem)
            place.start()
            place.wait()

    def loads(held, target, index):
        margin = 2 * HALO
        cols = pl.ds(0, piece + margin)
        if not (isinstance(index, int) and index == 0):
            cols = pl.ds(pl.multiple_of(index * piece + margin, HALO), piece)
        return [
            pltpu.make_async_copy(
                store.at[item, :, :, cols], block.at[:, :, cols], in_sems.at[row, index]
            )
            for row, (item, block) in enumerate(
                ((held * devices + me, own), (target, other))
            )
        ]

    def results(pair, index):
        held, slot = pair // SLOTS, pair % SLOTS
        cols = pl.ds(pl.multiple_of(index * piece, HALO), piece)
        return (
            pltpu.make_async_copy(
                ifg_block.at[:, :, cols], ifg.at[held, slot, :, :, cols], out_sems.at[0, index]
            ),
            pltpu.make_async_copy(
                coh_block.at[:, cols], coh.at[held, slot, :, cols], out_sems.at[1, index]
            ),
        )

    def leave(pair, index):
        for copy in results(pair, index):
            copy.start()

    def settle(last):
        @pl.when(last >= 0)
        def _():
            for index in range(pieces):
                for copy in results(jnp.maximum(last, 0), index):
                    copy.wait()

    def serve(pair, last):
        turn, ready = plan[TURN, pair], plan[READY, pair]
        due = (turn >= first) & (turn < after) & (ready > ready_above) & (ready <= ready_up_to) & (turn >= 0)

        @pl.when(due)
        def _():
            held = pair // SLOTS
            for index in range(pieces):
                for load in loads(held, plan[TARGET, pair], index):
                    load.start()
            settle(last)

            def arrive(index):
                for load in loads(held, plan[TARGET, pair], index):
                    load.wait()

            pair_sums(
                plan[WIDTH, pair], own, other, ifg_block, coh_block, main_band, edge_band,
                ((high_even, low_even), (high_odd, low_odd)), arrive,
                functools.partial(leave, pair),
            )

        return jnp.where(due, pair, last)

    settle(lax.fori_loop(0, slots, serve, jnp.int32(-1)))


def like(array):
    return jax.ShapeDtypeStruct(array.shape, array.dtype)


@functools.partial(jax.jit, static_argnames=("devices",))
def pair_work(plan, step, store, swapped, ifg, coh, devices):
    parts, lines, span = store.shape[1:]
    width = span - 2 * HALO
    tiles = width // TILE
    bf16 = jnp.bfloat16
    extra = [] if swapped is None else [swapped]
    placing = len(extra)
    return pl.pallas_call(
        functools.partial(pair_kernel, devices, bool(placing)),
        in_specs=[SMEM] * 2 + [ANYWHERE] + [VMEM] * placing + [ANYWHERE, ANYWHERE],
        out_specs=[ANYWHERE] * 3,
        scratch_shapes=[
            pltpu.VMEM((parts, lines, span), bf16),
            pltpu.VMEM((parts, lines, span), bf16),
            pltpu.VMEM((parts, lines, width), bf16),
            pltpu.VMEM((lines, width), bf16),
            pltpu.VMEM((TILE, TILE), bf16),
            pltpu.VMEM((TILE, TILE), bf16),
        ]
        + [pltpu.VMEM((group_of(tiles) + 2, ROWS, TILE), bf16)] * 4
        + [
            pltpu.SemaphoreType.DMA,
            pltpu.SemaphoreType.DMA((2, tiles // group_of(tiles))),
            pltpu.SemaphoreType.DMA((2, tiles // group_of(tiles))),
        ],
        out_shape=[like(store), like(ifg), like(coh)],
        input_output_aliases={2: 0, 3 + placing: 1, 4 + placing: 2},
        compiler_params=pltpu.CompilerParams(vmem_limit_bytes=VMEM_LIMIT),
        cost_estimate=pl.CostEstimate(
            flops=10_000_000_000, bytes_accessed=8_000_000, transcendentals=0
        ),
        name="pair_work",
    )(plan, step, store, *extra, ifg, coh)


def forward_kernel(ahead, keep, plan, step, _store, new, swapped, store, following, *refs):
    sems = refs[-1]
    now, core = step[4], plan[SELF, 0] % 2
    item, sent = plan[GET + core, now], plan[SEND + core, now + ahead]
    late = jnp.where(now > 0, plan[GET + 1 - core, jnp.maximum(now - 1, 0)], -1)
    moves = (
        (item >= 0, new, item, True),
        (late >= 0, swapped, late, True),
        ((sent >= 0) & (sent != item), following, sent, False),
    )

    def each(act):
        for index, (wanted, block, place, out) in enumerate(moves):

            @pl.when(wanted)
            def _():
                ends = (block, store.at[place]) if out else (store.at[place], block)
                act(pltpu.make_async_copy(*ends, sems.at[index]))

    each(lambda copy: copy.start())
    if keep:
        refs[0][...] = new[...]

    @pl.when((sent >= 0) & (sent == item))
    def _():
        following[...] = new[...]

    each(lambda copy: copy.wait())


@functools.partial(jax.jit, static_argnames=("ahead", "keep"))
def forward(plan, step, store, new, swapped, ahead, keep):
    return pl.pallas_call(
        functools.partial(forward_kernel, ahead, keep),
        in_specs=[SMEM] * 2 + [ANYWHERE, VMEM, VMEM],
        out_specs=[ANYWHERE, VMEM] + [VMEM] * keep,
        scratch_shapes=[pltpu.SemaphoreType.DMA((3,))],
        out_shape=[like(store)] + [like(new)] * (1 + keep),
        input_output_aliases={2: 0},
        compiler_params=pltpu.CompilerParams(vmem_limit_bytes=VMEM_LIMIT),
        name="forward",
    )(plan, step, store, new, swapped)


def shards(slc, partners, looks):
    devices = lax.axis_size("acq")
    me = lax.axis_index("acq").astype(jnp.int32)
    swap = [(d, d ^ 1) for d in range(devices)]
    stream = [(d, d - 2) for d in range(2, devices, 2)] + [(d, d + 2) for d in range(1, devices - 2, 2)]
    own, targets, widths = slc[:, 0], partners[:, 0], looks[:, 0]
    table = targets
    distance = 1
    while distance < devices:
        other = lax.ppermute(table, "acq", [(d, d ^ distance) for d in range(devices)])
        table = jnp.concatenate([table, other])
        distance *= 2

    count = lax.axis_size("rng")
    forth = [(i, i + 1) for i in range(count - 1)]
    back = [(target, source) for source, target in forth]
    before = lax.ppermute(own[..., -HALO:], "rng", forth)
    after = lax.ppermute(own[..., :HALO], "rng", back)
    edges = jnp.stack([before, after], axis=1)
    sibling = lax.ppermute(own, "acq", swap)
    sibling_edges = lax.ppermute(edges, "acq", swap)
    store, plan, send, after, ifg, coh = prepare(
        own, edges, sibling, sibling_edges, table, widths, me[None], devices
    )
    rounds = plan[ROUNDS, 0]
    late = jnp.int32(1 << 20)

    def pairs_of(now, store, ifg, coh):
        step = jnp.stack([jnp.int32(now), jnp.int32(now + 1), -late, late, jnp.int32(now)])
        return pair_work(plan, step, store, None, ifg, coh, devices=devices)

    def forwarded(now, store, new, swapped, ahead, keep=False):
        step = jnp.stack([jnp.int32(0)] * 4 + [jnp.int32(now)])
        return forward(plan, step, store, new, swapped, ahead=ahead, keep=keep)

    def hop(send):
        return lax.ppermute(send, "acq", stream)

    def swapped_with(got):
        return lax.ppermute(got, "acq", swap)

    def body(state):
        now, store, send, got, ifg, coh = state
        new, swapped = hop(send), swapped_with(got)
        store, ifg, coh = pairs_of(now, store, ifg, coh)
        store, send, got = forwarded(now, store, new, swapped, 1, True)
        return now + 1, store, send, got, ifg, coh

    def stepped(now, store, send, new, swapped, ifg, coh):
        got, new = new, hop(send)
        store, send = forwarded(now - 1, store, got, swapped, 2)
        swapped = swapped_with(got)
        store, ifg, coh = pairs_of(now, store, ifg, coh)
        return store, send, new, swapped, ifg, coh

    new = hop(send)
    store, ifg, coh = pairs_of(0, store, ifg, coh)
    state = (store, after, new, send, ifg, coh)
    for now in range(1, FIXED_ROUNDS):
        state = stepped(now, *state)
    store, send, got, swapped, ifg, coh = state
    store, _ = forwarded(FIXED_ROUNDS - 1, store, got, swapped, 2)
    now, store, _, got, ifg, coh = lax.while_loop(
        lambda state: state[0] < rounds,
        body,
        (jnp.int32(FIXED_ROUNDS), store, send, got, ifg, coh),
    )
    swapped = swapped_with(got)
    step = jnp.stack([now, late, -late, now, now])
    store, ifg, coh = pair_work(plan, step, store, None, ifg, coh, devices=devices)
    step = jnp.stack([now, late, now, late, now])
    _, ifg, coh = pair_work(plan, step, store, swapped, ifg, coh, devices=devices)
    return ifg[:, None], coh[:, None]


def solution(mesh):
    return jax.shard_map(
        shards,
        mesh=mesh,
        in_specs=(P(None, "acq", None, "slab", "rng"), P(None, "acq", None), P(None, "acq", None)),
        out_specs=(P(None, "acq", None, None, "slab", "rng"), P(None, "acq", None, "slab", "rng")),
        check_vma=False,
    )
```

```python
import functools

import jax
import jax.numpy as jnp
from jax import lax
from jax.experimental import pallas as pl
from jax.experimental.pallas import tpu as pltpu
from jax.sharding import PartitionSpec as P

SLOTS = 4
AZ_HALF = 2
HALO = 128
TILE = 256
ROWS = 32
GROUP = 16
TINY = 1e-37
PER_ROUND = 1
FIXED_ROUNDS = 7
NEVER = 1e6
SEND, GET, TURN, READY, ROUNDS, TARGET, WIDTH, SELF = 0, 2, 4, 5, 6, 8, 9, 10
VMEM = pl.BlockSpec(memory_space=pltpu.VMEM)
SMEM = pl.BlockSpec(memory_space=pltpu.SMEM)
ANYWHERE = pl.BlockSpec(memory_space=pltpu.HBM)
VMEM_LIMIT = 40 * 1024 * 1024


def azimuth(field):
    lines = field.shape[0]
    line = lax.broadcasted_iota(jnp.int32, field.shape, 0)
    above = jnp.where(line >= 1, pltpu.roll(field, 1, 0), 0.0)
    pair = field + above
    ends = jnp.where(line >= 2, pair, jnp.where(line == 0, pltpu.roll(field, 1, 0), 0.0))
    return (pair + jnp.where(line >= 2, pltpu.roll(field, 2, 0), 0.0)) + pltpu.roll(ends, lines - 2, 0)


def split_sums(own_re, own_im, other_re, other_im):
    fields = (
        own_re * other_re + own_im * other_im,
        own_im * other_re - own_re * other_im,
        own_re * own_re + own_im * own_im,
        other_re * other_re + other_im * other_im,
    )
    sums = jnp.concatenate([azimuth(field) for field in fields], axis=0)
    high = sums.astype(jnp.bfloat16)
    low = (sums - high.astype(jnp.float32)).astype(jnp.bfloat16)
    return high, low


def bands(width):
    row = lax.broadcasted_iota(jnp.int32, (TILE, TILE), 0)
    col = lax.broadcasted_iota(jnp.int32, (TILE, TILE), 1)
    main = jnp.abs(row - col) <= width
    lane = row % HALO
    place = jnp.where(lane >= HALO // 2, lane - HALO, TILE + lane)
    edge = jnp.abs(place - col) <= width
    as_type = lambda mask: jnp.where(mask, 1.0, 0.0).astype(jnp.bfloat16)
    return as_type(main), as_type(edge)


def group_of(tiles):
    return min(GROUP, tiles // 2)


def cuts_of(steps):
    return sorted({0, 1, steps // 2, steps}), sorted({0, steps // 2, steps})


def pair_sums(
    width, own, other, ifg, coh, main_band, edge_band, buffers, arrive, leave
):
    f32, bf16 = jnp.float32, jnp.bfloat16
    span = own.shape[-1] - 2 * HALO
    tiles = span // TILE
    main_band[...], edge_band[...] = bands(width)
    group = group_of(tiles)
    steps = tiles // group
    rows = group * ROWS
    count = jnp.full((8, TILE), (2 * AZ_HALF + 1) * (2 * width + 1), jnp.int32)
    scale = 1.0 / count.astype(f32)
    upper = lax.broadcasted_iota(jnp.int32, (group, ROWS, HALO), 2) >= HALO // 2
    dot = functools.partial(jnp.dot, preferred_element_type=f32)

    def place(start, size):
        return pl.ds(pl.multiple_of(start, HALO), size)

    def loaded(start, size):
        cols = place(start, size)
        return split_sums(
            *(ref[part, :, cols].astype(f32) for ref in (own, other) for part in (0, 1))
        )

    def fill(step, slot):
        high, low = buffers[slot]
        base = step * group * TILE
        high[0, :, HALO:], low[0, :, HALO:] = loaded(base, HALO)
        for tile in range(group):
            high[tile + 1], low[tile + 1] = loaded(base + HALO + tile * TILE, TILE)
        end = loaded(base + HALO + group * TILE, HALO)
        high[group + 1, :, :HALO], low[group + 1, :, :HALO] = end

    def spread(step, slot):
        high, low = buffers[slot]
        edge = jnp.concatenate(
            [jnp.where(upper, ref[:group, :, HALO:], ref[2:, :, :HALO]) for ref in (high, low)],
            axis=-1,
        )
        total = (
            dot(high[1 : group + 1].reshape(rows, TILE), main_band[...])
            + dot(low[1 : group + 1].reshape(rows, TILE), main_band[...])
            + dot(edge.reshape(rows, TILE), edge_band[...])
        ).reshape(group, 4, ROWS // 4, TILE)
        for tile in range(group):
            real, imag, power, other_power = (total[tile, field] for field in range(4))
            cols = place((step * group + tile) * TILE, TILE)
            ifg[0, :, cols] = (real * scale).astype(bf16)
            ifg[1, :, cols] = (imag * scale).astype(bf16)
            square = real * real + imag * imag
            size = square * lax.rsqrt(jnp.maximum(square, TINY))
            ratio = size * lax.rsqrt(power * other_power + 1e-06)
            coh[:, cols] = ratio.astype(bf16)

    def turn(step, slot, more=True):
        if more:
            arrive(step + 1)
            spread(step, slot)
            fill(step + 1, 1 - slot)
        else:
            spread(step, slot)
        leave(step)

    arrive(0)
    fill(0, 0)

    def twice(half, carry):
        turn(2 * half, 0)
        turn(2 * half + 1, 1)
        return carry

    lax.fori_loop(0, steps // 2 - 1, twice, 0)
    turn(steps - 2, 0)
    turn(steps - 1, 1, False)


def prepare_kernel(
    devices, table, widths, position, own_image, own_edges, sibling, sibling_edges, store, plan,
    send, after, ifg, coh, own, zero, load_sem, sems, zero_sems,
):
    me = position[0]
    chip, core = me // 2, me % 2
    held, span = own.shape[0], own.shape[-1]
    slots = held * SLOTS
    load = pltpu.make_async_copy(own_image, own, load_sem)
    load.start()
    zero[...] = jnp.zeros_like(zero)

    def clear(act):
        for slot in range(slots):

            @pl.when(table[slot // SLOTS, slot % SLOTS] < 0)
            def _():
                for ref, source, sem in ((ifg, zero, 0), (coh, zero.at[0], 1)):
                    place = ref.at[slot // SLOTS, slot % SLOTS]
                    act(pltpu.make_async_copy(source, place, zero_sems.at[slot, sem]))

    clear(lambda copy: copy.start())
    copies = []
    for index in range(held):
        for image, edges, owner in (
            (own, own_edges, me),
            (sibling, sibling_edges, me + 1 - 2 * core),
        ):
            place = store.at[index * devices + owner]
            for source, start, size in (
                (image.at[index], HALO, span),
                (edges.at[index, 0], 0, HALO),
                (edges.at[index, 1], HALO + span, HALO),
            ):
                copies.append(
                    pltpu.make_async_copy(
                        source, place.at[:, :, pl.ds(start, size)], sems.at[len(copies)]
                    )
                )
    load.wait()
    for copy in copies:
        copy.start()

    f32 = jnp.float32
    shape = (8, 128)
    row = lax.broadcasted_iota(jnp.int32, shape, 0)
    lane = lax.broadcasted_iota(jnp.int32, shape, 1)
    rowf, lanef = row.astype(f32), lane.astype(f32)
    home = ((lane % devices) // 2).astype(f32)
    nearest = jnp.full(shape, NEVER, f32)
    farthest = jnp.full(shape, -1.0, f32)
    for block in range(devices):
        holder = jnp.full(shape, (me ^ block) // 2, jnp.int32).astype(f32)
        hit = jnp.zeros(shape, jnp.bool_)
        for entry in range(slots):
            line, slot = block * held + entry // SLOTS, entry % SLOTS
            hit = hit | (lane == table[line, slot])
        nearest = jnp.where(hit, jnp.minimum(nearest, holder), nearest)
        farthest = jnp.where(hit, jnp.maximum(farthest, holder), farthest)
    need_down = (nearest < rowf) & (rowf <= home)
    need_up = (home < rowf) & (rowf <= farthest)
    key_down = nearest * 128 + lanef
    key_up = (devices - farthest) * 128 + lanef

    def move(need, key, ready, turn, items, now, towards):
        open_key = jnp.where(ready <= now, key, NEVER)
        best = jnp.min(open_key, axis=1, keepdims=True)
        chosen = (open_key == best) & (open_key < NEVER)
        item = jnp.max(jnp.where(chosen, lanef, -1.0), axis=1, keepdims=True)
        items = jnp.where(lanef == now, item, items)
        turn = jnp.where(chosen, now, turn)
        later = pltpu.roll(jnp.where(chosen, now + 2, NEVER), towards, 0)
        ready = jnp.where(chosen, NEVER, ready)
        ready = jnp.where(need, jnp.minimum(ready, later), ready)
        return ready, turn, items

    def advance(state):
        now, _, ready_down, turn_down, items_down, ready_up, turn_up, items_up = state
        ready_down, turn_down, items_down = move(
            need_down, key_down, ready_down, turn_down, items_down, now, 7
        )
        ready_up, turn_up, items_up = move(
            need_up, key_up, ready_up, turn_up, items_up, now, 1
        )
        soonest = jnp.min(jnp.minimum(ready_down, ready_up))
        return (now + 1.0, soonest) + (
            ready_down, turn_down, items_down, ready_up, turn_up, items_up
        )

    none = jnp.full(shape, -1.0, f32)
    ready_down = jnp.where(need_down & (rowf == home), 0.0, NEVER)
    ready_up = jnp.where(need_up & (rowf == home + 1), 0.0, NEVER)
    soonest = jnp.min(jnp.minimum(ready_down, ready_up))
    rounds, _, _, turn_down, items_down, _, turn_up, items_up = lax.while_loop(
        lambda state: state[1] < NEVER,
        advance,
        (jnp.float32(0.0), soonest, ready_down, none, none, ready_up, none, none),
    )

    def line_of(values, index):
        return jnp.max(jnp.where(row == index, values, -1.0), axis=0, keepdims=True)

    send_down, get_down = line_of(items_down, chip), line_of(items_down, chip + 1)
    send_up, get_up = line_of(items_up, chip + 1), line_of(items_up, chip)
    down_turn, up_turn = line_of(turn_down, chip + 1), line_of(turn_up, chip)
    lag = lambda turn, mine: jnp.where(turn >= 0, turn + jnp.where(mine, 1.0, 2.0), 0.0)
    arrival = jnp.maximum(lag(down_turn, core == 0), lag(up_turn, core == 1))
    partner = jnp.full(shape, -1, jnp.int32)
    for slot in range(slots):
        partner = jnp.where(row == slot, table[slot // SLOTS, slot % SLOTS], partner)
    ready = jnp.max(jnp.where(lane == partner, arrival, 0.0), axis=1, keepdims=True)
    ready = jnp.broadcast_to(ready, shape)

    def turned(values):
        return jnp.sum(jnp.where(row == lane, values, 0.0), axis=0, keepdims=True)

    ready_q = turned(ready)
    live_q = turned(jnp.where(partner >= 0, 1.0, 0.0)) > 0
    ahead = (ready_q < ready) | ((ready_q == ready) & (lane < row))
    rank = jnp.sum(jnp.where(ahead & live_q, 1.0, 0.0), axis=1, keepdims=True)
    rank = jnp.broadcast_to(rank, shape)
    gap = (rank - turned(rank)) / PER_ROUND
    whole = jnp.floor(gap)
    queue = (gap >= 0) & (gap == whole) & live_q
    turn = jnp.max(jnp.where(queue, ready_q + whole, 0.0), axis=1, keepdims=True)
    turn = turned(jnp.where(partner >= 0, turn, -1.0))
    result = jnp.full(shape, rounds, f32)
    for index, values in enumerate([send_down, send_up, get_down, get_up, turn, ready_q]):
        result = jnp.where(row == index, values, result)
    extra = jnp.full(shape, me, jnp.int32)
    for slot in range(slots):
        spot = slot // SLOTS, slot % SLOTS
        extra = jnp.where((row == TARGET - 8) & (lane == slot), table[spot], extra)
        extra = jnp.where((row == WIDTH - 8) & (lane == slot), widths[spot], extra)
    plan[:8] = result.astype(jnp.int32)
    plan[8:] = extra

    for copy in copies:
        copy.wait()
    sends = []
    for index, block in enumerate((send, after)):
        mine = jnp.where(core == 0, send_down, send_up)
        item = jnp.max(jnp.where(lane[:1] == index, mine, -1.0)).astype(jnp.int32)
        sends.append(
            pltpu.make_async_copy(
                store.at[jnp.where(item < 0, me, item)], block, sems.at[index]
            )
        )
    for copy in sends:
        copy.start()
    for copy in sends:
        copy.wait()
    clear(lambda copy: copy.wait())


def prepare(own, own_edges, sibling, sibling_edges, table, widths, position, devices):
    held, parts, lines, span = own.shape
    bf16 = jnp.bfloat16
    item = jax.ShapeDtypeStruct((parts, lines, span + 2 * HALO), bf16)
    return pl.pallas_call(
        functools.partial(prepare_kernel, devices),
        in_specs=[SMEM, SMEM, SMEM, ANYWHERE, VMEM, VMEM, VMEM],
        out_specs=[ANYWHERE, VMEM, VMEM, VMEM] + [ANYWHERE] * 2,
        scratch_shapes=[
            pltpu.VMEM(own.shape, bf16),
            pltpu.VMEM((parts, lines, span), bf16),
            pltpu.SemaphoreType.DMA,
            pltpu.SemaphoreType.DMA((6 * held,)),
            pltpu.SemaphoreType.DMA((held * SLOTS, 2)),
        ],
        out_shape=[
            jax.ShapeDtypeStruct((held * devices,) + item.shape, bf16),
            jax.ShapeDtypeStruct((16, 128), jnp.int32),
            item,
            item,
            jax.ShapeDtypeStruct((held, SLOTS, parts, lines, span), bf16),
            jax.ShapeDtypeStruct((held, SLOTS, lines, span), bf16),
        ],
        compiler_params=pltpu.CompilerParams(vmem_limit_bytes=VMEM_LIMIT),
        name="prepare",
    )(table, widths, position, own, own_edges, sibling, sibling_edges)


def pair_kernel(devices, placing, plan, step, _store, *refs):
    swapped = None
    if placing:
        swapped, *refs = refs
    (
        _ifg, _coh, store, ifg, coh, own, other, ifg_block, coh_block, main_band, edge_band,
        high_even, low_even, high_odd, low_odd, place_sem, in_sems, out_sems,
    ) = refs
    first, after, ready_above, ready_up_to, now = (step[index] for index in range(5))
    me = plan[SELF, 0]
    slots = ifg.shape[0] * SLOTS
    tiles = ifg.shape[-1] // TILE
    piece = group_of(tiles) * TILE
    steps = tiles * TILE // piece
    in_cuts, out_cuts = cuts_of(steps)

    if placing:
        item = jnp.where(now > 0, plan[GET + 1 - me % 2, jnp.maximum(now - 1, 0)], -1)

        @pl.when(item >= 0)
        def _():
            place = pltpu.make_async_copy(swapped, store.at[item], place_sem)
            place.start()
            place.wait()

    def loads(held, target, index):
        start, end = (cut * piece + 2 * HALO * (cut > 0) for cut in in_cuts[index : index + 2])
        cols = pl.ds(start, end - start)
        return [
            pltpu.make_async_copy(
                store.at[item, :, :, cols], block.at[:, :, cols], in_sems.at[row, index]
            )
            for row, (item, block) in enumerate(
                ((held * devices + me, own), (target, other))
            )
        ]

    def results(pair, index):
        held, slot = pair // SLOTS, pair % SLOTS
        start, end = (cut * piece for cut in out_cuts[index : index + 2])
        cols = pl.ds(start, end - start)
        return (
            pltpu.make_async_copy(
                ifg_block.at[:, :, cols], ifg.at[held, slot, :, :, cols], out_sems.at[0, index]
            ),
            pltpu.make_async_copy(
                coh_block.at[:, cols], coh.at[held, slot, :, cols], out_sems.at[1, index]
            ),
        )

    def when_equal(step, place, act):
        if isinstance(step, int):
            if step == place:
                act()
        else:
            pl.when(step == place)(act)

    def settle(last):
        @pl.when(last >= 0)
        def _():
            for index in range(len(out_cuts) - 1):
                for copy in results(jnp.maximum(last, 0), index):
                    copy.wait()

    def serve(pair, last):
        turn, ready = plan[TURN, pair], plan[READY, pair]
        due = (turn >= first) & (turn < after) & (ready > ready_above) & (ready <= ready_up_to) & (turn >= 0)

        @pl.when(due)
        def _():
            held = pair // SLOTS
            for index in range(len(in_cuts) - 1):
                for load in loads(held, plan[TARGET, pair], index):
                    load.start()
            settle(last)

            def arrive(step):
                for index in range(len(in_cuts) - 1):

                    def wait():
                        for load in loads(held, plan[TARGET, pair], index):
                            load.wait()

                    when_equal(step, in_cuts[index], wait)

            def leave(step):
                for index in range(len(out_cuts) - 1):

                    def start():
                        for copy in results(pair, index):
                            copy.start()

                    when_equal(step, out_cuts[index + 1] - 1, start)

            pair_sums(
                plan[WIDTH, pair], own, other, ifg_block, coh_block, main_band, edge_band,
                ((high_even, low_even), (high_odd, low_odd)), arrive,
                leave,
            )

        return jnp.where(due, pair, last)

    settle(lax.fori_loop(0, slots, serve, jnp.int32(-1)))


def like(array):
    return jax.ShapeDtypeStruct(array.shape, array.dtype)


@functools.partial(jax.jit, static_argnames=("devices",))
def pair_work(plan, step, store, swapped, ifg, coh, devices):
    parts, lines, span = store.shape[1:]
    width = span - 2 * HALO
    tiles = width // TILE
    bf16 = jnp.bfloat16
    extra = [] if swapped is None else [swapped]
    placing = len(extra)
    return pl.pallas_call(
        functools.partial(pair_kernel, devices, bool(placing)),
        in_specs=[SMEM] * 2 + [ANYWHERE] + [VMEM] * placing + [ANYWHERE, ANYWHERE],
        out_specs=[ANYWHERE] * 3,
        scratch_shapes=[
            pltpu.VMEM((parts, lines, span), bf16),
            pltpu.VMEM((parts, lines, span), bf16),
            pltpu.VMEM((parts, lines, width), bf16),
            pltpu.VMEM((lines, width), bf16),
            pltpu.VMEM((TILE, TILE), bf16),
            pltpu.VMEM((TILE, TILE), bf16),
        ]
        + [pltpu.VMEM((group_of(tiles) + 2, ROWS, TILE), bf16)] * 4
        + [
            pltpu.SemaphoreType.DMA,
            pltpu.SemaphoreType.DMA((2, 3)),
            pltpu.SemaphoreType.DMA((2, 2)),
        ],
        out_shape=[like(store), like(ifg), like(coh)],
        input_output_aliases={2: 0, 3 + placing: 1, 4 + placing: 2},
        compiler_params=pltpu.CompilerParams(vmem_limit_bytes=VMEM_LIMIT),
        cost_estimate=pl.CostEstimate(
            flops=10_000_000_000, bytes_accessed=8_000_000, transcendentals=0
        ),
        name="pair_work",
    )(plan, step, store, *extra, ifg, coh)


def forward_kernel(ahead, keep, plan, step, _store, new, swapped, store, following, *refs):
    sems = refs[-1]
    now, core = step[4], plan[SELF, 0] % 2
    item, sent = plan[GET + core, now], plan[SEND + core, now + ahead]
    late = jnp.where(now > 0, plan[GET + 1 - core, jnp.maximum(now - 1, 0)], -1)
    moves = (
        (item >= 0, new, item, True),
        (late >= 0, swapped, late, True),
        ((sent >= 0) & (sent != item), following, sent, False),
    )

    def each(act):
        for index, (wanted, block, place, out) in enumerate(moves):

            @pl.when(wanted)
            def _():
                ends = (block, store.at[place]) if out else (store.at[place], block)
                act(pltpu.make_async_copy(*ends, sems.at[index]))

    each(lambda copy: copy.start())
    if keep:
        refs[0][...] = new[...]

    @pl.when((sent >= 0) & (sent == item))
    def _():
        following[...] = new[...]

    each(lambda copy: copy.wait())


@functools.partial(jax.jit, static_argnames=("ahead", "keep"))
def forward(plan, step, store, new, swapped, ahead, keep):
    return pl.pallas_call(
        functools.partial(forward_kernel, ahead, keep),
        in_specs=[SMEM] * 2 + [ANYWHERE, VMEM, VMEM],
        out_specs=[ANYWHERE, VMEM] + [VMEM] * keep,
        scratch_shapes=[pltpu.SemaphoreType.DMA((3,))],
        out_shape=[like(store)] + [like(new)] * (1 + keep),
        input_output_aliases={2: 0},
        compiler_params=pltpu.CompilerParams(vmem_limit_bytes=VMEM_LIMIT),
        name="forward",
    )(plan, step, store, new, swapped)


def shards(slc, partners, looks):
    devices = lax.axis_size("acq")
    me = lax.axis_index("acq").astype(jnp.int32)
    swap = [(d, d ^ 1) for d in range(devices)]
    stream = [(d, d - 2) for d in range(2, devices, 2)] + [(d, d + 2) for d in range(1, devices - 2, 2)]
    own, targets, widths = slc[:, 0], partners[:, 0], looks[:, 0]
    table = targets
    distance = 1
    while distance < devices:
        other = lax.ppermute(table, "acq", [(d, d ^ distance) for d in range(devices)])
        table = jnp.concatenate([table, other])
        distance *= 2

    count = lax.axis_size("rng")
    forth = [(i, i + 1) for i in range(count - 1)]
    back = [(target, source) for source, target in forth]
    before = lax.ppermute(own[..., -HALO:], "rng", forth)
    after = lax.ppermute(own[..., :HALO], "rng", back)
    edges = jnp.stack([before, after], axis=1)
    sibling = lax.ppermute(own, "acq", swap)
    sibling_edges = lax.ppermute(edges, "acq", swap)
    store, plan, send, after, ifg, coh = prepare(
        own, edges, sibling, sibling_edges, table, widths, me[None], devices
    )
    rounds = plan[ROUNDS, 0]
    late = jnp.int32(1 << 20)

    def pairs_of(now, store, ifg, coh):
        step = jnp.stack([jnp.int32(now), jnp.int32(now + 1), -late, late, jnp.int32(now)])
        return pair_work(plan, step, store, None, ifg, coh, devices=devices)

    def forwarded(now, store, new, swapped, ahead, keep=False):
        step = jnp.stack([jnp.int32(0)] * 4 + [jnp.int32(now)])
        return forward(plan, step, store, new, swapped, ahead=ahead, keep=keep)

    def hop(send):
        return lax.ppermute(send, "acq", stream)

    def swapped_with(got):
        return lax.ppermute(got, "acq", swap)

    def body(state):
        now, store, send, got, ifg, coh = state
        new, swapped = hop(send), swapped_with(got)
        store, ifg, coh = pairs_of(now, store, ifg, coh)
        store, send, got = forwarded(now, store, new, swapped, 1, True)
        return now + 1, store, send, got, ifg, coh

    def stepped(now, store, send, new, swapped, ifg, coh):
        got, new = new, hop(send)
        store, send = forwarded(now - 1, store, got, swapped, 2)
        store, ifg, coh = pairs_of(now, store, ifg, coh)
        got, coh = lax.optimization_barrier((got, coh))
        return store, send, new, swapped_with(got), ifg, coh

    new = hop(send)
    store, ifg, coh = pairs_of(0, store, ifg, coh)
    state = (store, after, new, send, ifg, coh)
    for now in range(1, FIXED_ROUNDS):
        state = stepped(now, *state)
    store, send, got, swapped, ifg, coh = state
    store, _ = forwarded(FIXED_ROUNDS - 1, store, got, swapped, 2)
    now, store, _, got, ifg, coh = lax.while_loop(
        lambda state: state[0] < rounds,
        body,
        (jnp.int32(FIXED_ROUNDS), store, send, got, ifg, coh),
    )
    swapped = swapped_with(got)
    step = jnp.stack([now, late, -late, now, now])
    store, ifg, coh = pair_work(plan, step, store, None, ifg, coh, devices=devices)
    step = jnp.stack([now, late, now, late, now])
    _, ifg, coh = pair_work(plan, step, store, swapped, ifg, coh, devices=devices)
    return ifg[:, None], coh[:, None]


def solution(mesh):
    return jax.shard_map(
        shards,
        mesh=mesh,
        in_specs=(P(None, "acq", None, "slab", "rng"), P(None, "acq", None), P(None, "acq", None)),
        out_specs=(P(None, "acq", None, None, "slab", "rng"), P(None, "acq", None, "slab", "rng")),
        check_vma=False,
    )
```

```python
import functools

import jax
import jax.numpy as jnp
from jax import lax
from jax.experimental import pallas as pl
from jax.experimental.pallas import tpu as pltpu
from jax.sharding import PartitionSpec as P

SLOTS = 4
AZ_HALF = 2
HALO = 128
TILE = 256
ROWS = 32
GROUP = 16
TINY = 1e-37
PER_ROUND = 1
FIXED_ROUNDS = 8
NEVER = 1e6
SEND, GET, TURN, READY, ROUNDS, TARGET, WIDTH, SELF = 0, 2, 4, 5, 6, 8, 9, 10
VMEM = pl.BlockSpec(memory_space=pltpu.VMEM)
SMEM = pl.BlockSpec(memory_space=pltpu.SMEM)
ANYWHERE = pl.BlockSpec(memory_space=pltpu.HBM)
VMEM_LIMIT = 40 * 1024 * 1024


def azimuth(field):
    lines = field.shape[0]
    line = lax.broadcasted_iota(jnp.int32, field.shape, 0)
    above = jnp.where(line >= 1, pltpu.roll(field, 1, 0), 0.0)
    pair = field + above
    ends = jnp.where(line >= 2, pair, jnp.where(line == 0, pltpu.roll(field, 1, 0), 0.0))
    return (pair + jnp.where(line >= 2, pltpu.roll(field, 2, 0), 0.0)) + pltpu.roll(ends, lines - 2, 0)


def split_sums(own_re, own_im, other_re, other_im):
    fields = (
        own_re * other_re + own_im * other_im,
        own_im * other_re - own_re * other_im,
        own_re * own_re + own_im * own_im,
        other_re * other_re + other_im * other_im,
    )
    sums = jnp.concatenate([azimuth(field) for field in fields], axis=0)
    high = sums.astype(jnp.bfloat16)
    low = (sums - high.astype(jnp.float32)).astype(jnp.bfloat16)
    return high, low


def bands(width):
    row = lax.broadcasted_iota(jnp.int32, (TILE, TILE), 0)
    col = lax.broadcasted_iota(jnp.int32, (TILE, TILE), 1)
    main = jnp.abs(row - col) <= width
    lane = row % HALO
    place = jnp.where(lane >= HALO // 2, lane - HALO, TILE + lane)
    edge = jnp.abs(place - col) <= width
    as_type = lambda mask: jnp.where(mask, 1.0, 0.0).astype(jnp.bfloat16)
    return as_type(main), as_type(edge)


def group_of(tiles):
    return min(GROUP, tiles // 2)


def cuts_of(steps):
    return sorted({0, 1, steps // 2, steps}), sorted({0, steps // 2, steps})


def pair_sums(
    width, own, other, ifg, coh, main_band, edge_band, buffers, arrive, leave
):
    f32, bf16 = jnp.float32, jnp.bfloat16
    span = own.shape[-1] - 2 * HALO
    tiles = span // TILE
    main_band[...], edge_band[...] = bands(width)
    group = group_of(tiles)
    steps = tiles // group
    rows = group * ROWS
    count = jnp.full((8, TILE), (2 * AZ_HALF + 1) * (2 * width + 1), jnp.int32)
    scale = 1.0 / count.astype(f32)
    upper = lax.broadcasted_iota(jnp.int32, (group, ROWS, HALO), 2) >= HALO // 2
    dot = functools.partial(jnp.dot, preferred_element_type=f32)

    def place(start, size):
        return pl.ds(pl.multiple_of(start, HALO), size)

    def loaded(start, size):
        cols = place(start, size)
        return split_sums(
            *(ref[part, :, cols].astype(f32) for ref in (own, other) for part in (0, 1))
        )

    def fill(step, slot):
        high, low = buffers[slot]
        base = step * group * TILE
        high[0, :, HALO:], low[0, :, HALO:] = loaded(base, HALO)
        for tile in range(group):
            high[tile + 1], low[tile + 1] = loaded(base + HALO + tile * TILE, TILE)
        end = loaded(base + HALO + group * TILE, HALO)
        high[group + 1, :, :HALO], low[group + 1, :, :HALO] = end

    def spread(step, slot):
        high, low = buffers[slot]
        edge = jnp.concatenate(
            [jnp.where(upper, ref[:group, :, HALO:], ref[2:, :, :HALO]) for ref in (high, low)],
            axis=-1,
        )
        total = (
            dot(high[1 : group + 1].reshape(rows, TILE), main_band[...])
            + dot(low[1 : group + 1].reshape(rows, TILE), main_band[...])
            + dot(edge.reshape(rows, TILE), edge_band[...])
        ).reshape(group, 4, ROWS // 4, TILE)
        for tile in range(group):
            real, imag, power, other_power = (total[tile, field] for field in range(4))
            cols = place((step * group + tile) * TILE, TILE)
            ifg[0, :, cols] = (real * scale).astype(bf16)
            ifg[1, :, cols] = (imag * scale).astype(bf16)
            square = real * real + imag * imag
            size = square * lax.rsqrt(jnp.maximum(square, TINY))
            ratio = size * lax.rsqrt(power * other_power + 1e-06)
            coh[:, cols] = ratio.astype(bf16)

    def turn(step, slot, more=True):
        if more:
            arrive(step + 1)
            spread(step, slot)
            fill(step + 1, 1 - slot)
        else:
            spread(step, slot)
        leave(step)

    arrive(0)
    fill(0, 0)

    def twice(half, carry):
        turn(2 * half, 0)
        turn(2 * half + 1, 1)
        return carry

    lax.fori_loop(0, steps // 2 - 1, twice, 0)
    turn(steps - 2, 0)
    turn(steps - 1, 1, False)


def prepare_kernel(
    devices, table, widths, position, own_image, own_edges, sibling, sibling_edges, store, plan,
    send, after, ifg, coh, own, zero, load_sem, sems, zero_sems,
):
    me = position[0]
    chip, core = me // 2, me % 2
    held, span = own.shape[0], own.shape[-1]
    slots = held * SLOTS
    load = pltpu.make_async_copy(own_image, own, load_sem)
    load.start()
    zero[...] = jnp.zeros_like(zero)

    def clear(act):
        for slot in range(slots):

            @pl.when(table[slot // SLOTS, slot % SLOTS] < 0)
            def _():
                for ref, source, sem in ((ifg, zero, 0), (coh, zero.at[0], 1)):
                    place = ref.at[slot // SLOTS, slot % SLOTS]
                    act(pltpu.make_async_copy(source, place, zero_sems.at[slot, sem]))

    clear(lambda copy: copy.start())
    copies = []
    for index in range(held):
        for image, edges, owner in (
            (own, own_edges, me),
            (sibling, sibling_edges, me + 1 - 2 * core),
        ):
            place = store.at[index * devices + owner]
            for source, start, size in (
                (image.at[index], HALO, span),
                (edges.at[index, 0], 0, HALO),
                (edges.at[index, 1], HALO + span, HALO),
            ):
                copies.append(
                    pltpu.make_async_copy(
                        source, place.at[:, :, pl.ds(start, size)], sems.at[len(copies)]
                    )
                )
    load.wait()
    for copy in copies:
        copy.start()

    f32 = jnp.float32
    shape = (8, 128)
    row = lax.broadcasted_iota(jnp.int32, shape, 0)
    lane = lax.broadcasted_iota(jnp.int32, shape, 1)
    rowf, lanef = row.astype(f32), lane.astype(f32)
    home = ((lane % devices) // 2).astype(f32)
    nearest = jnp.full(shape, NEVER, f32)
    farthest = jnp.full(shape, -1.0, f32)
    for block in range(devices):
        holder = jnp.full(shape, (me ^ block) // 2, jnp.int32).astype(f32)
        hit = jnp.zeros(shape, jnp.bool_)
        for entry in range(slots):
            line, slot = block * held + entry // SLOTS, entry % SLOTS
            hit = hit | (lane == table[line, slot])
        nearest = jnp.where(hit, jnp.minimum(nearest, holder), nearest)
        farthest = jnp.where(hit, jnp.maximum(farthest, holder), farthest)
    need_down = (nearest < rowf) & (rowf <= home)
    need_up = (home < rowf) & (rowf <= farthest)
    key_down = nearest * 128 + lanef
    key_up = (devices - farthest) * 128 + lanef

    def move(need, key, ready, turn, items, now, towards):
        open_key = jnp.where(ready <= now, key, NEVER)
        best = jnp.min(open_key, axis=1, keepdims=True)
        chosen = (open_key == best) & (open_key < NEVER)
        item = jnp.max(jnp.where(chosen, lanef, -1.0), axis=1, keepdims=True)
        items = jnp.where(lanef == now, item, items)
        turn = jnp.where(chosen, now, turn)
        later = pltpu.roll(jnp.where(chosen, now + 2, NEVER), towards, 0)
        ready = jnp.where(chosen, NEVER, ready)
        ready = jnp.where(need, jnp.minimum(ready, later), ready)
        return ready, turn, items

    def advance(state):
        now, _, ready_down, turn_down, items_down, ready_up, turn_up, items_up = state
        ready_down, turn_down, items_down = move(
            need_down, key_down, ready_down, turn_down, items_down, now, 7
        )
        ready_up, turn_up, items_up = move(
            need_up, key_up, ready_up, turn_up, items_up, now, 1
        )
        soonest = jnp.min(jnp.minimum(ready_down, ready_up))
        return (now + 1.0, soonest) + (
            ready_down, turn_down, items_down, ready_up, turn_up, items_up
        )

    none = jnp.full(shape, -1.0, f32)
    ready_down = jnp.where(need_down & (rowf == home), 0.0, NEVER)
    ready_up = jnp.where(need_up & (rowf == home + 1), 0.0, NEVER)
    soonest = jnp.min(jnp.minimum(ready_down, ready_up))
    rounds, _, _, turn_down, items_down, _, turn_up, items_up = lax.while_loop(
        lambda state: state[1] < NEVER,
        advance,
        (jnp.float32(0.0), soonest, ready_down, none, none, ready_up, none, none),
    )

    def line_of(values, index):
        return jnp.max(jnp.where(row == index, values, -1.0), axis=0, keepdims=True)

    send_down, get_down = line_of(items_down, chip), line_of(items_down, chip + 1)
    send_up, get_up = line_of(items_up, chip + 1), line_of(items_up, chip)
    down_turn, up_turn = line_of(turn_down, chip + 1), line_of(turn_up, chip)
    lag = lambda turn, mine: jnp.where(turn >= 0, turn + jnp.where(mine, 1.0, 2.0), 0.0)
    arrival = jnp.maximum(lag(down_turn, core == 0), lag(up_turn, core == 1))
    partner = jnp.full(shape, -1, jnp.int32)
    for slot in range(slots):
        partner = jnp.where(row == slot, table[slot // SLOTS, slot % SLOTS], partner)
    ready = jnp.max(jnp.where(lane == partner, arrival, 0.0), axis=1, keepdims=True)
    ready = jnp.broadcast_to(ready, shape)

    def turned(values):
        return jnp.sum(jnp.where(row == lane, values, 0.0), axis=0, keepdims=True)

    ready_q = turned(ready)
    live_q = turned(jnp.where(partner >= 0, 1.0, 0.0)) > 0
    ahead = (ready_q < ready) | ((ready_q == ready) & (lane < row))
    rank = jnp.sum(jnp.where(ahead & live_q, 1.0, 0.0), axis=1, keepdims=True)
    rank = jnp.broadcast_to(rank, shape)
    gap = (rank - turned(rank)) / PER_ROUND
    whole = jnp.floor(gap)
    queue = (gap >= 0) & (gap == whole) & live_q
    turn = jnp.max(jnp.where(queue, ready_q + whole, 0.0), axis=1, keepdims=True)
    turn = turned(jnp.where(partner >= 0, turn, -1.0))
    result = jnp.full(shape, rounds, f32)
    for index, values in enumerate([send_down, send_up, get_down, get_up, turn, ready_q]):
        result = jnp.where(row == index, values, result)
    extra = jnp.full(shape, me, jnp.int32)
    for slot in range(slots):
        spot = slot // SLOTS, slot % SLOTS
        extra = jnp.where((row == TARGET - 8) & (lane == slot), table[spot], extra)
        extra = jnp.where((row == WIDTH - 8) & (lane == slot), widths[spot], extra)
    plan[:8] = result.astype(jnp.int32)
    plan[8:] = extra

    for copy in copies:
        copy.wait()
    sends = []
    for index, block in enumerate((send, after)):
        mine = jnp.where(core == 0, send_down, send_up)
        item = jnp.max(jnp.where(lane[:1] == index, mine, -1.0)).astype(jnp.int32)
        sends.append(
            pltpu.make_async_copy(
                store.at[jnp.where(item < 0, me, item)], block, sems.at[index]
            )
        )
    for copy in sends:
        copy.start()
    for copy in sends:
        copy.wait()
    clear(lambda copy: copy.wait())


def prepare(own, own_edges, sibling, sibling_edges, table, widths, position, devices):
    held, parts, lines, span = own.shape
    bf16 = jnp.bfloat16
    item = jax.ShapeDtypeStruct((parts, lines, span + 2 * HALO), bf16)
    return pl.pallas_call(
        functools.partial(prepare_kernel, devices),
        in_specs=[SMEM, SMEM, SMEM, ANYWHERE, VMEM, VMEM, VMEM],
        out_specs=[ANYWHERE, VMEM, VMEM, VMEM] + [ANYWHERE] * 2,
        scratch_shapes=[
            pltpu.VMEM(own.shape, bf16),
            pltpu.VMEM((parts, lines, span), bf16),
            pltpu.SemaphoreType.DMA,
            pltpu.SemaphoreType.DMA((6 * held,)),
            pltpu.SemaphoreType.DMA((held * SLOTS, 2)),
        ],
        out_shape=[
            jax.ShapeDtypeStruct((held * devices,) + item.shape, bf16),
            jax.ShapeDtypeStruct((16, 128), jnp.int32),
            item,
            item,
            jax.ShapeDtypeStruct((held, SLOTS, parts, lines, span), bf16),
            jax.ShapeDtypeStruct((held, SLOTS, lines, span), bf16),
        ],
        compiler_params=pltpu.CompilerParams(vmem_limit_bytes=VMEM_LIMIT),
        name="prepare",
    )(table, widths, position, own, own_edges, sibling, sibling_edges)


def pair_kernel(devices, placing, plan, step, _store, *refs):
    swapped = None
    if placing:
        swapped, *refs = refs
    (
        _ifg, _coh, store, ifg, coh, own, other, ifg_block, coh_block, main_band, edge_band,
        high_even, low_even, high_odd, low_odd, place_sem, in_sems, out_sems,
    ) = refs
    first, after, ready_above, ready_up_to, now = (step[index] for index in range(5))
    me = plan[SELF, 0]
    slots = ifg.shape[0] * SLOTS
    tiles = ifg.shape[-1] // TILE
    piece = group_of(tiles) * TILE
    steps = tiles * TILE // piece
    in_cuts, out_cuts = cuts_of(steps)

    if placing:
        item = jnp.where(now > 0, plan[GET + 1 - me % 2, jnp.maximum(now - 1, 0)], -1)

        @pl.when(item >= 0)
        def _():
            place = pltpu.make_async_copy(swapped, store.at[item], place_sem)
            place.start()
            place.wait()

    def loads(held, target, index):
        start, end = (cut * piece + 2 * HALO * (cut > 0) for cut in in_cuts[index : index + 2])
        cols = pl.ds(start, end - start)
        return [
            pltpu.make_async_copy(
                store.at[item, :, :, cols], block.at[:, :, cols], in_sems.at[row, index]
            )
            for row, (item, block) in enumerate(
                ((held * devices + me, own), (target, other))
            )
        ]

    def results(pair, index):
        held, slot = pair // SLOTS, pair % SLOTS
        start, end = (cut * piece for cut in out_cuts[index : index + 2])
        cols = pl.ds(start, end - start)
        return (
            pltpu.make_async_copy(
                ifg_block.at[:, :, cols], ifg.at[held, slot, :, :, cols], out_sems.at[0, index]
            ),
            pltpu.make_async_copy(
                coh_block.at[:, cols], coh.at[held, slot, :, cols], out_sems.at[1, index]
            ),
        )

    def when_equal(step, place, act):
        if isinstance(step, int):
            if step == place:
                act()
        else:
            pl.when(step == place)(act)

    def settle(last):
        @pl.when(last >= 0)
        def _():
            for index in range(len(out_cuts) - 1):
                for copy in results(jnp.maximum(last, 0), index):
                    copy.wait()

    def serve(pair, last):
        turn, ready = plan[TURN, pair], plan[READY, pair]
        due = (turn >= first) & (turn < after) & (ready > ready_above) & (ready <= ready_up_to) & (turn >= 0)

        @pl.when(due)
        def _():
            held = pair // SLOTS
            for index in range(len(in_cuts) - 1):
                for load in loads(held, plan[TARGET, pair], index):
                    load.start()
            settle(last)

            def arrive(step):
                for index in range(len(in_cuts) - 1):

                    def wait():
                        for load in loads(held, plan[TARGET, pair], index):
                            load.wait()

                    when_equal(step, in_cuts[index], wait)

            def leave(step):
                for index in range(len(out_cuts) - 1):

                    def start():
                        for copy in results(pair, index):
                            copy.start()

                    when_equal(step, out_cuts[index + 1] - 1, start)

            pair_sums(
                plan[WIDTH, pair], own, other, ifg_block, coh_block, main_band, edge_band,
                ((high_even, low_even), (high_odd, low_odd)), arrive,
                leave,
            )

        return jnp.where(due, pair, last)

    settle(lax.fori_loop(0, slots, serve, jnp.int32(-1)))


def like(array):
    return jax.ShapeDtypeStruct(array.shape, array.dtype)


@functools.partial(jax.jit, static_argnames=("devices",))
def pair_work(plan, step, store, swapped, ifg, coh, devices):
    parts, lines, span = store.shape[1:]
    width = span - 2 * HALO
    tiles = width // TILE
    bf16 = jnp.bfloat16
    extra = [] if swapped is None else [swapped]
    placing = len(extra)
    return pl.pallas_call(
        functools.partial(pair_kernel, devices, bool(placing)),
        in_specs=[SMEM] * 2 + [ANYWHERE] + [VMEM] * placing + [ANYWHERE, ANYWHERE],
        out_specs=[ANYWHERE] * 3,
        scratch_shapes=[
            pltpu.VMEM((parts, lines, span), bf16),
            pltpu.VMEM((parts, lines, span), bf16),
            pltpu.VMEM((parts, lines, width), bf16),
            pltpu.VMEM((lines, width), bf16),
            pltpu.VMEM((TILE, TILE), bf16),
            pltpu.VMEM((TILE, TILE), bf16),
        ]
        + [pltpu.VMEM((group_of(tiles) + 2, ROWS, TILE), bf16)] * 4
        + [
            pltpu.SemaphoreType.DMA,
            pltpu.SemaphoreType.DMA((2, 3)),
            pltpu.SemaphoreType.DMA((2, 2)),
        ],
        out_shape=[like(store), like(ifg), like(coh)],
        input_output_aliases={2: 0, 3 + placing: 1, 4 + placing: 2},
        compiler_params=pltpu.CompilerParams(vmem_limit_bytes=VMEM_LIMIT),
        cost_estimate=pl.CostEstimate(
            flops=10_000_000_000, bytes_accessed=8_000_000, transcendentals=0
        ),
        name="pair_work",
    )(plan, step, store, *extra, ifg, coh)


def forward_kernel(ahead, keep, plan, step, _store, new, swapped, store, following, *refs):
    sems = refs[-1]
    now, core = step[4], plan[SELF, 0] % 2
    item, sent = plan[GET + core, now], plan[SEND + core, now + ahead]
    late = jnp.where(now > 0, plan[GET + 1 - core, jnp.maximum(now - 1, 0)], -1)
    moves = (
        (item >= 0, new, item, True),
        (late >= 0, swapped, late, True),
        ((sent >= 0) & (sent != item), following, sent, False),
    )

    def each(act):
        for index, (wanted, block, place, out) in enumerate(moves):

            @pl.when(wanted)
            def _():
                ends = (block, store.at[place]) if out else (store.at[place], block)
                act(pltpu.make_async_copy(*ends, sems.at[index]))

    each(lambda copy: copy.start())
    if keep:
        refs[0][...] = new[...]

    @pl.when((sent >= 0) & (sent == item))
    def _():
        following[...] = new[...]

    each(lambda copy: copy.wait())


@functools.partial(jax.jit, static_argnames=("ahead", "keep"))
def forward(plan, step, store, new, swapped, ahead, keep):
    return pl.pallas_call(
        functools.partial(forward_kernel, ahead, keep),
        in_specs=[SMEM] * 2 + [ANYWHERE, VMEM, VMEM],
        out_specs=[ANYWHERE, VMEM] + [VMEM] * keep,
        scratch_shapes=[pltpu.SemaphoreType.DMA((3,))],
        out_shape=[like(store)] + [like(new)] * (1 + keep),
        input_output_aliases={2: 0},
        compiler_params=pltpu.CompilerParams(vmem_limit_bytes=VMEM_LIMIT),
        name="forward",
    )(plan, step, store, new, swapped)


def shards(slc, partners, looks):
    devices = lax.axis_size("acq")
    me = lax.axis_index("acq").astype(jnp.int32)
    swap = [(d, d ^ 1) for d in range(devices)]
    stream = [(d, d - 2) for d in range(2, devices, 2)] + [(d, d + 2) for d in range(1, devices - 2, 2)]
    own, targets, widths = slc[:, 0], partners[:, 0], looks[:, 0]
    table = targets
    distance = 1
    while distance < devices:
        other = lax.ppermute(table, "acq", [(d, d ^ distance) for d in range(devices)])
        table = jnp.concatenate([table, other])
        distance *= 2

    count = lax.axis_size("rng")
    forth = [(i, i + 1) for i in range(count - 1)]
    back = [(target, source) for source, target in forth]
    before = lax.ppermute(own[..., -HALO:], "rng", forth)
    after = lax.ppermute(own[..., :HALO], "rng", back)
    edges = jnp.stack([before, after], axis=1)
    sibling = lax.ppermute(own, "acq", swap)
    sibling_edges = lax.ppermute(edges, "acq", swap)
    store, plan, send, after, ifg, coh = prepare(
        own, edges, sibling, sibling_edges, table, widths, me[None], devices
    )
    rounds = plan[ROUNDS, 0]
    late = jnp.int32(1 << 20)

    def pairs_of(now, store, ifg, coh):
        step = jnp.stack([jnp.int32(now), jnp.int32(now + 1), -late, late, jnp.int32(now)])
        return pair_work(plan, step, store, None, ifg, coh, devices=devices)

    def forwarded(now, store, new, swapped, ahead, keep=False):
        step = jnp.stack([jnp.int32(0)] * 4 + [jnp.int32(now)])
        return forward(plan, step, store, new, swapped, ahead=ahead, keep=keep)

    def hop(send):
        return lax.ppermute(send, "acq", stream)

    def swapped_with(got):
        return lax.ppermute(got, "acq", swap)

    def body(state):
        now, store, send, got, ifg, coh = state
        new, swapped = hop(send), swapped_with(got)
        store, ifg, coh = pairs_of(now, store, ifg, coh)
        store, send, got = forwarded(now, store, new, swapped, 1, True)
        return now + 1, store, send, got, ifg, coh

    def stepped(now, store, send, new, swapped, ifg, coh):
        got, new = new, hop(send)
        store, send = forwarded(now - 1, store, got, swapped, 2)
        store, ifg, coh = pairs_of(now, store, ifg, coh)
        got, coh = lax.optimization_barrier((got, coh))
        return store, send, new, swapped_with(got), ifg, coh

    new = hop(send)
    store, ifg, coh = pairs_of(0, store, ifg, coh)
    state = (store, after, new, send, ifg, coh)
    for now in range(1, FIXED_ROUNDS):
        state = stepped(now, *state)
    store, send, got, swapped, ifg, coh = state
    store, _ = forwarded(FIXED_ROUNDS - 1, store, got, swapped, 2)
    now, store, _, got, ifg, coh = lax.while_loop(
        lambda state: state[0] < rounds,
        body,
        (jnp.int32(FIXED_ROUNDS), store, send, got, ifg, coh),
    )
    swapped = swapped_with(got)
    step = jnp.stack([now, late, -late, now, now])
    store, ifg, coh = pair_work(plan, step, store, None, ifg, coh, devices=devices)
    step = jnp.stack([now, late, now, late, now])
    _, ifg, coh = pair_work(plan, step, store, swapped, ifg, coh, devices=devices)
    return ifg[:, None], coh[:, None]


def solution(mesh):
    return jax.shard_map(
        shards,
        mesh=mesh,
        in_specs=(P(None, "acq", None, "slab", "rng"), P(None, "acq", None), P(None, "acq", None)),
        out_specs=(P(None, "acq", None, None, "slab", "rng"), P(None, "acq", None, "slab", "rng")),
        check_vma=False,
    )
```
